32 devices in a mesh: ctx: 8 (over z, core), tp: 4 (over y, x).
Axes of the slice: x: 2, y: 2, z: 4, core: 2. Of those that a mesh axis runs over, the one named last changes fastest.
Arguments:
- inner_x: bfloat16 [2, 1024, 16384], P(None, 'ctx', 'tp'), may hold values from -6 to 6
- gate_z: bfloat16 [2, 1024, 16384], P(None, 'ctx', 'tp'), may hold values from -6 to 6
- proj_bc: bfloat16 [2, 1024, 8, 512], P(None, 'ctx', 'tp'), may hold values from -6 to 6
- dt_raw: float32 [2, 256, 1024], P(None, 'tp', 'ctx'), may hold values from -6 to 41
- a_log: float32 [256], P('tp'), may hold values from -10 to 1
- dt_bias: float32 [256], P('tp'), may hold values from -0.5 to 0.5
- d_skip: float32 [256], P('tp'), may hold values from 0.5 to 1.5
- conv_x: float32 [4, 16384], P(None, 'tp'), may hold values from -3 to 3
- conv_bc: float32 [4, 8, 512], P(None, 'tp'), may hold values from -3 to 3
- bias_x: float32 [16384], P('tp'), may hold values from -0.5 to 0.5
- bias_bc: float32 [8, 512], P('tp'), may hold values from -0.5 to 0.5
- norm_gain: float32 [16384], P('tp'), may hold values from 0.25 to 1.75
- init_state: float32 [2, 256, 64, 256], P(None, 'tp'), may hold values from -6 to 6
- init_conv_x: bfloat16 [2, 3, 16384], P(None, None, 'tp'), may hold values from -6 to 6
- init_conv_bc: bfloat16 [2, 3, 8, 512], P(None, None, 'tp'), may hold values from -6 to 6
- lengths: int32 [2], replicated, may hold values from 512 to 1024, as said below
- dec_x: bfloat16 [4, 64, 16384], P(None, 'ctx', 'tp'), may hold values from -6 to 6
- dec_z: bfloat16 [4, 64, 16384], P(None, 'ctx', 'tp'), may hold values from -6 to 6
- dec_bc: bfloat16 [4, 64, 8, 512], P(None, 'ctx', 'tp'), may hold values from -6 to 6
- dec_dt: float32 [4, 256, 64], P(None, 'tp', 'ctx'), may hold values from -2.5 to 1
- row_prompt: int32 [64], P('ctx'), may hold values from 0 to 1
- w_out: bfloat16 [16384, 8192], P('tp', 'ctx'), may hold values from -0.046875 to 0.046875
Outputs:
- prefill_out: bfloat16 [2, 1024, 16384], P(None, 'ctx', 'tp')
- layer_out: bfloat16 [4, 64, 8192], P(None, 'tp', 'ctx')
The draws below stay inside these ranges and needn't reach their ends.
Inputs may be any that keep to these rules, and one draw needn't show every extreme that they name: Positions from lengths[s] on are padding of prompt s. At least one prompt has all 1024 positions live.
All inputs are finite; a program needn't handle non-finite values.
Results may differ from the reference program's by a relative error of at most 0.005.
Values may be sent and summed in bfloat16 or wider, within the bound.
No kernel may reach another device: no remote copies, remote signals or barrier semaphores. Data moves between devices by JAX's collectives and lax.ppermute only.
A program may use at most 256 MiB of HBM per device.

```python
import math
import jax
import jax.numpy as jnp
from jax import lax

D = 8192
HEADS = 256
HEAD_DIM = 64
STATE = 256
GROUPS = 8
CONV_K = 4
SEQS = 2
TOK_DEV = 128
STEPS = 4
INNER = 16384
LENGTH = 1024
ROWS = 64


def draw_a_log(key, part):
    first, second, third = jax.random.split(jax.random.fold_in(key, 11), 3)
    share = 0.6
    slow = jax.random.uniform(first, (HEADS,)) < share
    slow_rate = jnp.exp(jax.random.uniform(second, (HEADS,), minval=jnp.log(0.05), maxval=jnp.log(0.3))) / (0.02 * LENGTH)
    fast_rate = jax.random.uniform(third, (HEADS,), minval=1.0, maxval=1.65)
    return jnp.log(jnp.where(slow, slow_rate, fast_rate)).astype(jnp.float32)


def draw_dt_raw(key, part):
    first, second, third, fourth = jax.random.split(jax.random.fold_in(key, 23), 4)
    spread = 0.7
    noise = jax.random.uniform(first, (SEQS, HEADS, LENGTH), minval=-spread, maxval=spread)
    blocks = LENGTH // TOK_DEV
    offset = jnp.repeat(jax.random.uniform(second, (SEQS, HEADS, blocks), minval=-0.35, maxval=0.35), TOK_DEV, axis=2)
    places = jax.random.randint(third, (SEQS, 3), 0, LENGTH)
    spot = jnp.any(jnp.arange(LENGTH)[None, None, :] == places[:, :, None], axis=1)
    height = 0.02 * LENGTH * (1.0 + jax.random.uniform(fourth, (SEQS, 1, LENGTH)))
    base = -3.9 + noise + offset
    return jnp.where(spot[:, None, :], height, base).astype(jnp.float32)


def draw_lengths(key, part):
    first, second = jax.random.split(jax.random.fold_in(key, 31), 2)
    full_one = jax.random.randint(first, (), 0, SEQS)
    others = jax.random.randint(second, (SEQS,), LENGTH // 2, LENGTH + 1)
    chosen = jnp.arange(SEQS, dtype=jnp.int32) == full_one
    return jnp.where(chosen, LENGTH, others).astype(jnp.int32)


def with_ends(entries, key, low, top_value):
    index_at = [jax.random.randint(jax.random.fold_in(key, axis), (), 0, length) for axis, length in enumerate(entries.shape)]
    widest = entries.shape.index(max(entries.shape))
    beside = index_at[:widest] + [(index_at[widest] + 1) % entries.shape[widest]] + index_at[widest + 1:]
    return entries.at[tuple(index_at)].set(low).at[tuple(beside)].set(top_value)


def level_of(own_key, dims, cuts, least, largest):
    factor_of, own = 1.0, jax.random.fold_in(own_key, 6)
    for axis_at, parts in cuts:
        heights = jnp.exp(jax.random.uniform(jax.random.fold_in(own, axis_at), (parts,), jnp.float32, least / len(cuts), largest / len(cuts)))
        factor_of = factor_of * jnp.repeat(heights, dims[axis_at] // parts).reshape([-1 if axis == axis_at else 1 for axis in range(len(dims))])
    return factor_of


def bell_draw(own_key, shape, deviation, most, cuts=(), kind=jnp.bfloat16):
    values = deviation * jax.random.normal(own_key, shape, jnp.float32)
    if cuts:
        values = values * level_of(own_key, shape, cuts, -0.22, 0.18)
    return jnp.clip(values, -most, most).astype(kind)


def setup_inputs(seed: int = 0) -> dict:
    streams_of = jax.random.split(jax.random.key(seed), 23)
    inner_x = bell_draw(streams_of[0], (SEQS, LENGTH, INNER), 1.0, 6.0, ((1, 8), (2, 4)))
    gate_z = bell_draw(streams_of[1], (SEQS, LENGTH, INNER), 1.0, 6.0, ((1, 8), (2, 4)))
    proj_bc = bell_draw(streams_of[2], (SEQS, LENGTH, GROUPS, 2 * STATE), 1.0, 6.0, ((1, 8), (2, 4)))
    dt_raw = draw_dt_raw(jax.random.fold_in(streams_of[22], 71), 0)
    a_log = draw_a_log(jax.random.fold_in(streams_of[22], 71), 0)
    dt_bias = jnp.clip(jax.random.uniform(streams_of[5], (HEADS,), jnp.float32, -0.5, 0.5) * level_of(streams_of[5], (HEADS,), ((0, 4),), -0.4, 0.0), -0.5, 0.5)
    d_skip = jnp.clip(0.5 + 1.0 * jax.random.uniform(streams_of[6], (HEADS,), jnp.float32) ** level_of(streams_of[6], (HEADS,), ((0, 4),), -0.2, 0.2), 0.5, 1.5)
    conv_x = bell_draw(streams_of[7], (CONV_K, INNER), CONV_K ** -0.5, 3.0, ((1, 4),), jnp.float32)
    conv_bc = bell_draw(streams_of[8], (CONV_K, GROUPS, 2 * STATE), CONV_K ** -0.5, 3.0, ((1, 4),), jnp.float32)
    bias_x = jnp.clip(jax.random.uniform(streams_of[9], (INNER,), jnp.float32, -0.5, 0.5) * level_of(streams_of[9], (INNER,), ((0, 4),), -0.4, 0.0), -0.5, 0.5)
    bias_bc = jnp.clip(jax.random.uniform(streams_of[10], (GROUPS, 2 * STATE), jnp.float32, -0.5, 0.5) * level_of(streams_of[10], (GROUPS, 2 * STATE), ((0, 4),), -0.4, 0.0), -0.5, 0.5)
    norm_gain = jnp.clip(1.0 + 0.15 * jax.random.normal(streams_of[11], (INNER,), jnp.float32), 0.25, 1.75)
    init_state = bell_draw(streams_of[12], (SEQS, HEADS, HEAD_DIM, STATE), 1.0, 6.0, ((1, 4),), jnp.float32)
    init_conv_x = bell_draw(streams_of[13], (SEQS, CONV_K - 1, INNER), 1.0, 6.0, ((2, 4),))
    init_conv_bc = bell_draw(streams_of[14], (SEQS, CONV_K - 1, GROUPS, 2 * STATE), 1.0, 6.0, ((2, 4),))
    lengths = draw_lengths(jax.random.fold_in(streams_of[22], 71), 0)
    dec_x = bell_draw(streams_of[16], (STEPS, ROWS, INNER), 1.0, 6.0, ((1, 8), (2, 4)))
    dec_z = bell_draw(streams_of[17], (STEPS, ROWS, INNER), 1.0, 6.0, ((1, 8), (2, 4)))
    dec_bc = bell_draw(streams_of[18], (STEPS, ROWS, GROUPS, 2 * STATE), 1.0, 6.0, ((1, 8), (2, 4)))
    dec_dt = jnp.clip(-2.5 + 3.5 * jax.random.uniform(streams_of[19], (STEPS, HEADS, ROWS), jnp.float32) ** level_of(streams_of[19], (STEPS, HEADS, ROWS), ((1, 4), (2, 8)), -0.2, 0.2), -2.5, 1.0)
    row_prompt = with_ends(jax.random.randint(streams_of[20], (ROWS,), 0, SEQS), jax.random.fold_in(streams_of[20], 1), 0, SEQS - 1).astype(jnp.int32)
    w_out = bell_draw(streams_of[21], (INNER, D), INNER ** -0.5, 0.046875, ((0, 4), (1, 8)))
    return dict(inner_x=inner_x, gate_z=gate_z, proj_bc=proj_bc, dt_raw=dt_raw, a_log=a_log, dt_bias=dt_bias, d_skip=d_skip, conv_x=conv_x, conv_bc=conv_bc, bias_x=bias_x, bias_bc=bias_bc, norm_gain=norm_gain, init_state=init_state, init_conv_x=init_conv_x, init_conv_bc=init_conv_bc, lengths=lengths, dec_x=dec_x, dec_z=dec_z, dec_bc=dec_bc, dec_dt=dec_dt, row_prompt=row_prompt, w_out=w_out)


epsilon = 1e-05
highest = lax.Precision.HIGHEST

def gated_norm(values, gate, gain):
    mixed = values * jax.nn.silu(gate)
    shape = mixed.shape
    grouped = mixed.reshape(shape[:-1] + (GROUPS, shape[-1] // GROUPS))
    scaled = grouped * lax.rsqrt(lax.optimization_barrier(jnp.mean(grouped * grouped, axis=-1, keepdims=True)) + epsilon)
    return scaled.reshape(shape) * gain

def prefill_prompt(inner_row, gate_row, bc_row, raw_rate, start_state, start_x, start_bc, length, a_log, dt_bias, d_skip, tap_weights, tap_bias, norm_gain):
    head_part = jnp.concatenate([start_x, start_bc.reshape(CONV_K - 1, -1)], axis=-1)
    body_part = jnp.concatenate([inner_row, bc_row.reshape(LENGTH, -1)], axis=-1)
    raw = jnp.concatenate([head_part, body_part], axis=0)
    padded = raw.astype(jnp.float32)
    total = tap_bias
    for offset in range(CONV_K):
        total = total + tap_weights[offset] * padded[offset:offset + LENGTH]
    active = jax.nn.silu(total)
    per_group = HEADS // GROUPS
    block = math.gcd(LENGTH, 256)
    count = LENGTH // block
    values = active[:, :INNER].reshape(count, block, GROUPS, per_group, HEAD_DIM)
    mixers = active[:, INNER:].reshape(count, block, GROUPS, 2 * STATE)
    live = (jnp.arange(LENGTH, dtype=jnp.int32) < length).astype(jnp.float32)
    rate = jnp.exp(a_log)
    step_size = jax.nn.softplus(raw_rate + dt_bias[:, None]) * live[None, :]
    log_decay = -rate[:, None] * step_size
    step_blocks = step_size.reshape(GROUPS, per_group, count, block).transpose(2, 0, 1, 3)
    decay_blocks = log_decay.reshape(GROUPS, per_group, count, block).transpose(2, 0, 1, 3)
    lower = jnp.arange(block)[:, None] >= jnp.arange(block)[None, :]
    skip_group = d_skip.reshape(GROUPS, per_group)

    def advance(state, items):
        value_block, mixer_block, step_block, decay_block = items
        b_part = mixer_block[..., :STATE]
        c_part = mixer_block[..., STATE:]
        running = jnp.cumsum(decay_block, axis=-1)
        scores = jnp.einsum('tgn,ugn->gtu', c_part, b_part, precision=highest)
        gap = running[..., :, None] - running[..., None, :]
        mixing = jnp.where(lower, jnp.exp(jnp.where(lower, gap, 0.0)), 0.0) * scores[:, None] * step_block[..., None, :]
        y_local = jnp.einsum('ghtu,ughp->tghp', mixing, value_block, precision=highest)
        y_carried = jnp.einsum('tgn,ghpn->tghp', c_part, state, precision=highest) * jnp.exp(jnp.transpose(running, (2, 0, 1)))[..., None]
        to_end = jnp.exp(running[..., -1:] - running) * step_block
        weighted = value_block * jnp.transpose(to_end, (2, 0, 1))[..., None]
        new_state = jnp.exp(running[..., -1])[..., None, None] * state + jnp.einsum('ughp,ugn->ghpn', weighted, b_part, precision=highest)
        return (new_state, y_local + y_carried + skip_group[:, :, None] * value_block)
    final, outputs = lax.scan(advance, start_state.reshape(GROUPS, per_group, HEAD_DIM, STATE), (values, mixers, step_blocks, decay_blocks))
    mixed_y = outputs.reshape(LENGTH, INNER)
    result = gated_norm(mixed_y, gate_row.astype(jnp.float32), norm_gain).astype(jnp.bfloat16)
    tail = lax.dynamic_slice_in_dim(raw, length.astype(jnp.int32), CONV_K - 1, 0).astype(jnp.float32)
    return (result, final, tail)

def reference(inner_x, gate_z, proj_bc, dt_raw, a_log, dt_bias, d_skip, conv_x, conv_bc, bias_x, bias_bc, norm_gain, init_state, init_conv_x, init_conv_bc, lengths, dec_x, dec_z, dec_bc, dec_dt, row_prompt, w_out):
    tap_weights = jnp.concatenate([conv_x, conv_bc.reshape(CONV_K, -1)], axis=-1)
    tap_bias = jnp.concatenate([bias_x, bias_bc.reshape(-1)], axis=-1)
    results, finals, tails = ([], [], [])
    for prompt in range(SEQS):
        result, final, tail = prefill_prompt(inner_x[prompt], gate_z[prompt], proj_bc[prompt], dt_raw[prompt], init_state[prompt], init_conv_x[prompt], init_conv_bc[prompt], lengths[prompt], a_log, dt_bias, d_skip, tap_weights, tap_bias, norm_gain)
        results.append(result)
        finals.append(final)
        tails.append(tail)
    prefill_out = jnp.stack(results)
    final_all = jnp.stack(finals)
    tail_all = jnp.stack(tails)
    per_group = HEADS // GROUPS
    rate_group = jnp.exp(a_log).reshape(GROUPS, per_group)
    skip_group = d_skip.reshape(GROUPS, per_group)

    def decode_row(items):
        prompt, row_x, row_z, row_bc, row_dt = items
        state = lax.dynamic_index_in_dim(final_all, prompt.astype(jnp.int32), 0, keepdims=False)
        window = lax.dynamic_index_in_dim(tail_all, prompt.astype(jnp.int32), 0, keepdims=False)
        hidden = []
        for moment in range(STEPS):
            fresh = jnp.concatenate([row_x[moment], row_bc[moment].reshape(-1)]).astype(jnp.float32)
            full = jnp.concatenate([window, fresh[None]], axis=0)
            total = tap_bias
            for offset in range(CONV_K):
                total = total + tap_weights[offset] * full[offset]
            active = jax.nn.silu(total)
            values = active[:INNER].reshape(GROUPS, per_group, HEAD_DIM)
            mixers = active[INNER:].reshape(GROUPS, 2 * STATE)
            step_row = jax.nn.softplus(row_dt[moment] + dt_bias).reshape(GROUPS, per_group)
            keep = jnp.exp(-rate_group * step_row)
            state = keep[..., None, None] * state + (step_row[..., None] * values)[..., None] * mixers[:, None, None, :STATE]
            y_row = jnp.einsum('ghpn,gn->ghp', state, mixers[:, STATE:], precision=highest) + skip_group[:, :, None] * values
            hidden.append(gated_norm(y_row.reshape(INNER), row_z[moment].astype(jnp.float32), norm_gain).astype(jnp.bfloat16))
            window = full[1:]
        return jnp.stack(hidden)
    hidden_rows = lax.map(decode_row, (row_prompt, jnp.transpose(dec_x, (1, 0, 2)), jnp.transpose(dec_z, (1, 0, 2)), jnp.transpose(dec_bc, (1, 0, 2, 3)), jnp.transpose(dec_dt, (2, 0, 1))))
    dec_hidden = jnp.transpose(hidden_rows, (1, 0, 2))
    layer_out = jnp.dot(dec_hidden.reshape(-1, INNER), w_out, preferred_element_type=jnp.float32)
    return (prefill_out, layer_out.reshape(STEPS, ROWS, D).astype(jnp.bfloat16))
```

```python
import jax
import jax.numpy as jnp
from jax import lax
from jax.sharding import PartitionSpec as P

HEADS = 256
HEAD_DIM = 64
GROUPS = 8

epsilon = 1e-05
highest = lax.Precision.HIGHEST


def silu(v):
    return v * jax.nn.sigmoid(v)


def group_norm(values, gate, gain):
    mixed = values * silu(gate)
    scale = lax.rsqrt(jnp.mean(mixed * mixed, axis=-1, keepdims=True) + epsilon)
    return (mixed * scale * gain).astype(jnp.bfloat16)


def shards(
    inner_x,
    gate_z,
    proj_bc,
    dt_raw,
    a_log,
    dt_bias,
    d_skip,
    conv_x,
    conv_bc,
    bias_x,
    bias_bc,
    norm_gain,
    init_state,
    init_conv_x,
    init_conv_bc,
    lengths,
    dec_x,
    dec_z,
    dec_bc,
    dec_dt,
    row_prompt,
    w_out,
):
    f32, bf16 = jnp.float32, jnp.bfloat16
    prompts, tokens, width = inner_x.shape
    groups, pair = proj_bc.shape[2:]
    state_size = pair // 2
    heads = dt_raw.shape[1] // groups
    gwidth = width // groups
    hd = gwidth // heads
    taps = conv_x.shape[0]
    steps, batch = dec_x.shape[:2]
    cols = w_out.shape[1]
    n = lax.axis_size("ctx")
    tp = lax.axis_size("tp")
    assert groups in (1, 2) and n % groups == 0
    per = groups
    m = n // per
    device = lax.axis_index("ctx")
    u, c = device // per, device % per
    span_tokens = per * tokens
    rows_u = per * batch

    def mine(arr, axis):
        return lax.dynamic_index_in_dim(arr, c, axis, keepdims=False)

    def swap(arr):
        return lax.ppermute(arr, "ctx", [(i, i ^ 1) for i in range(n)])

    def in_order(own, other, axis):
        first = jnp.where(c == 0, own, other)
        second = jnp.where(c == 0, other, own)
        return jnp.concatenate([first, second], axis=axis)

    def pair_up(arr, gaxis, taxis):
        if per == 1:
            return jnp.squeeze(arr, gaxis)
        other = swap(lax.dynamic_index_in_dim(arr, 1 - c, gaxis, keepdims=False))
        return in_order(mine(arr, gaxis), other, taxis)

    def shift(arr, k):
        return lax.ppermute(
            arr, "ctx", [(i, (i + k * per) % n) for i in range(n)]
        )

    flat = jnp.concatenate([inner_x.reshape(prompts, tokens, groups, gwidth), proj_bc], axis=-1)
    wide = gwidth + pair
    rim = jnp.zeros((prompts, taps - 1, wide), bf16)
    for g in range(per):
        pairs = [(v * per + per - 1, (v + 1) * per + g) for v in range(m - 1)]
        got = lax.ppermute(flat[:, tokens - taps + 1 :, g], "ctx", pairs)
        rim = jnp.where(c == g, got, rim)
    places = device * tokens + jnp.arange(tokens, dtype=jnp.int32)
    target = lengths[:, None] - (taps - 1) + jnp.arange(taps - 1, dtype=jnp.int32)[None, :]
    picker = (places[None, None, :] == target[:, :, None]).astype(bf16)
    tails = lax.psum(
        jnp.einsum("sjt,stgc->sjgc", picker, flat, preferred_element_type=f32), "ctx"
    )
    raw = pair_up(flat, 2, 1)
    dt = pair_up(dt_raw.reshape(prompts, groups, heads, tokens), 1, 2)
    dec_flat = jnp.concatenate([dec_x.reshape(steps, batch, groups, gwidth), dec_bc], axis=-1)
    dec_raw = pair_up(dec_flat, 2, 1)
    dec_step = pair_up(dec_dt.reshape(steps, groups, heads, batch), 1, 2)
    dec_gate = pair_up(dec_z.reshape(steps, batch, groups, gwidth), 2, 1)
    prompt_of = row_prompt if per == 1 else in_order(row_prompt, swap(row_prompt), 0)
    gate = pair_up(gate_z.reshape(prompts, tokens, groups, gwidth), 2, 1)

    tap_w = jnp.concatenate(
        [mine(conv_x.reshape(taps, groups, gwidth), 1), mine(conv_bc, 1)], axis=-1
    )
    tap_b = jnp.concatenate([mine(bias_x.reshape(groups, gwidth), 0), mine(bias_bc, 0)])
    gain = mine(norm_gain.reshape(groups, gwidth), 0)
    rate = jnp.exp(mine(a_log.reshape(groups, heads), 0))
    dtb = mine(dt_bias.reshape(groups, heads), 0)
    skip = mine(d_skip.reshape(groups, heads), 0)
    start = mine(init_state.reshape(prompts, groups, heads, hd, state_size), 1)
    start_rim = jnp.concatenate(
        [mine(init_conv_x.reshape(prompts, taps - 1, groups, gwidth), 2), mine(init_conv_bc, 2)],
        axis=-1,
    )

    padded = jnp.concatenate([jnp.where(u == 0, start_rim, rim), raw], axis=1).astype(f32)
    total = tap_b
    for k in range(taps):
        total = total + tap_w[k] * padded[:, k : k + span_tokens]
    active = silu(total)
    values = active[..., :gwidth].reshape(prompts, span_tokens, heads, hd)
    b_part = active[..., gwidth : gwidth + state_size]
    c_part = active[..., gwidth + state_size :]
    at = u * span_tokens + jnp.arange(span_tokens, dtype=jnp.int32)
    live = (at[None, :] < lengths[:, None]).astype(f32)
    step = jax.nn.softplus(dt + dtb[None, :, None]) * live[:, None, :]
    log_decay = -rate[None, :, None] * step
    upper = (jnp.arange(span_tokens)[:, None] <= jnp.arange(span_tokens)[None, :]).astype(f32)
    running = jnp.einsum("sht,tu->shu", log_decay, upper, precision=highest)
    span = running[..., -1]
    decay = jnp.exp(span)
    to_end = jnp.exp(running[..., -1:] - running) * step
    weighted = values * jnp.transpose(to_end, (0, 2, 1))[..., None]
    own = jnp.einsum("sthp,stn->shpn", weighted, b_part, precision=highest)
    own = own + jnp.where(u == 0, 1.0, 0.0) * decay[..., None, None] * start

    parts = 2 * prompts
    own_k = own.reshape(parts, -1, hd, state_size)
    decay_k = decay.reshape(parts, -1)
    arrived = []
    carry = jnp.zeros(own_k.shape[1:], bf16)
    along = [(i, i + per) for i in range(n - per)]
    for t in range(parts + m - 2):
        at_k = jnp.clip(t - u, 0, parts - 1)
        own_t = lax.dynamic_index_in_dim(own_k, at_k, 0, keepdims=False)
        decay_t = lax.dynamic_index_in_dim(decay_k, at_k, 0, keepdims=False)
        leave = (decay_t[:, None, None] * carry.astype(f32) + own_t).astype(bf16)
        carry = lax.ppermute(leave, "ctx", along)
        arrived.append(carry)

    dec_act_tail = mine(tails, 2)
    pick = (prompt_of[:, None] == jnp.arange(prompts, dtype=jnp.int32)[None, :]).astype(f32)
    window = jnp.einsum("rs,sjc->jrc", pick, dec_act_tail, precision=highest)
    full = jnp.concatenate([window, dec_raw.astype(f32)], axis=0)
    total = tap_b
    for k in range(taps):
        total = total + tap_w[k] * full[k : k + steps]
    dact = silu(total)
    xd = dact[..., :gwidth].reshape(steps, rows_u, heads, hd)
    bd = dact[..., gwidth : gwidth + state_size]
    cd = dact[..., gwidth + state_size :]
    stepd = jax.nn.softplus(jnp.transpose(dec_step, (0, 2, 1)) + dtb)
    logd = -rate * stepd
    upto = [logd[0]]
    for i in range(1, steps):
        upto.append(upto[-1] + logd[i])
    local = []
    for i in range(steps):
        y = skip[:, None] * xd[i]
        for j in range(i + 1):
            scale = jnp.sum(cd[i] * bd[j], axis=-1)[:, None] * jnp.exp(upto[i] - upto[j]) * stepd[j]
            y = y + scale[..., None] * xd[j]
        local.append(y)

    lanes = 128
    payload = jnp.concatenate(
        [
            jnp.concatenate(
                [
                    cd.reshape(steps * rows_u, state_size),
                    jnp.broadcast_to(
                        jnp.tile(prompt_of.astype(f32), steps)[:, None], (steps * rows_u, lanes)
                    ),
                ],
                axis=1,
            ),
            jnp.pad(span, ((0, 0), (0, state_size + lanes - heads))),
        ],
        axis=0,
    )
    blocks = [payload] + [shift(payload, k) for k in range(1, m)]
    after = jnp.zeros_like(span)
    for k in range(1, m):
        span_k = blocks[k][steps * rows_u :, :heads]
        after = after + jnp.where((u - k) % m > u, span_k, 0.0)
    asked = jnp.concatenate([b[: steps * rows_u] for b in blocks], axis=0)
    read = jnp.einsum("rn,shpn->srhp", asked[:, :state_size], own, precision=highest)
    read = read * jnp.exp(after)[:, None, :, None]
    chosen = read[0]
    for s in range(1, prompts):
        chosen = jnp.where(asked[:, state_size][:, None, None] == s, read[s], chosen)
    chosen = chosen.reshape(m, steps, rows_u, heads, hd)
    from_state = chosen[0]
    for k in range(1, m):
        from_state = from_state + shift(chosen[k].astype(bf16), -k).astype(f32)
    hidden = []
    for i in range(steps):
        y = jnp.exp(upto[i])[..., None] * from_state[i] + local[i]
        hidden.append(group_norm(y.reshape(rows_u, gwidth), dec_gate[i].astype(f32), gain))
    hidden = jnp.stack(hidden)
    got = jnp.stack([hidden] + [shift(hidden, k) for k in range(1, m)])
    got = jnp.concatenate([got[::-1], got[::-1]])
    got = lax.dynamic_slice_in_dim(got, m - 1 - u, m, 0)
    if per == 2:
        got = in_order(got, swap(got), 3)
    product = jnp.dot(
        jnp.swapaxes(got, 0, 1).reshape(-1, width), w_out, preferred_element_type=f32
    )
    terms = lax.all_to_all(product.reshape(steps, tp, -1, cols), "tp", 1, 1)
    layer_out = jnp.sum(terms, axis=1).astype(bf16)

    lower = jnp.arange(span_tokens)[:, None] >= jnp.arange(span_tokens)[None, :]
    outs = []
    per_prompt = parts // prompts
    for s in range(prompts):
        scores = jnp.einsum("tn,un->tu", c_part[s], b_part[s], precision=highest)
        gap = running[s][:, :, None] - running[s][:, None, :]
        mixing = (
            jnp.where(lower, jnp.exp(jnp.where(lower, gap, 0.0)), 0.0)
            * scores[None]
            * step[s][:, None, :]
        )
        y = jnp.einsum("htu,uhp->thp", mixing, values[s], precision=highest)
        y = y + skip[:, None] * values[s]
        first = s * per_prompt
        seen = jnp.stack(arrived[first : first + per_prompt + m - 2])
        entry = lax.dynamic_slice_in_dim(seen, jnp.maximum(u - 1, 0), per_prompt, 0)
        entry = entry.reshape(heads, hd, state_size)
        entry = jnp.where(u == 0, start[s], entry.astype(f32))
        grow = jnp.exp(jnp.transpose(running[s]))[..., None]
        y = y + jnp.einsum("tn,hpn->thp", c_part[s], entry, precision=highest) * grow
        out = group_norm(y.reshape(span_tokens, gwidth), gate[s].astype(f32), gain)
        if per == 2:
            out = out.reshape(per, tokens, gwidth)
            own_out = mine(out, 0)
            other = swap(lax.dynamic_index_in_dim(out, 1 - c, 0, keepdims=False))
            out = in_order(own_out, other, 1)
        outs.append(out)
    return (jnp.stack(outs), layer_out)


def solution(mesh):
    in_specs = (
        P(None, "ctx", "tp"),
        P(None, "ctx", "tp"),
        P(None, "ctx", "tp", None),
        P(None, "tp", "ctx"),
        P("tp"),
        P("tp"),
        P("tp"),
        P(None, "tp"),
        P(None, "tp", None),
        P("tp"),
        P("tp", None),
        P("tp"),
        P(None, "tp", None, None),
        P(None, None, "tp"),
        P(None, None, "tp", None),
        P(),
        P(None, "ctx", "tp"),
        P(None, "ctx", "tp"),
        P(None, "ctx", "tp", None),
        P(None, "tp", "ctx"),
        P("ctx"),
        P("tp", "ctx"),
    )
    out_specs = (P(None, "ctx", "tp"), P(None, "tp", "ctx"))
    return jax.shard_map(shards, mesh=mesh, in_specs=in_specs, out_specs=out_specs, check_vma=False)
```

```python
import functools

import jax
import jax.numpy as jnp
from jax import lax
from jax.experimental import pallas as pl
from jax.experimental.pallas import tpu as pltpu
from jax.sharding import PartitionSpec as P

epsilon = 1e-05
highest = lax.Precision.HIGHEST
f32, bf16 = jnp.float32, jnp.bfloat16
lanes = 128
vmem = 40 * 1024 * 1024


def silu(v):
    return v * (1.0 / (1.0 + jnp.exp(-v)))


def softplus(v):
    return jnp.maximum(v, 0.0) + jnp.log1p(jnp.exp(-jnp.abs(v)))


def exact(a, b):
    return jnp.dot(a, b, precision=highest, preferred_element_type=f32)


def exact_t(a, b):
    return lax.dot_general(
        a, b, (((1,), (1,)), ((), ())), precision=highest, preferred_element_type=f32
    )


def one_pass(a, b):
    return jnp.dot(a, b, preferred_element_type=f32)


def halves(a):
    high = a.astype(bf16)
    return high, (a - high.astype(f32)).astype(bf16)


def to_channels(columns, hd, first):
    row = lax.broadcasted_iota(jnp.int32, (lanes, columns), 0)
    col = lax.broadcasted_iota(jnp.int32, (lanes, columns), 1)
    return (row == col // hd + first).astype(f32)


def joined(refs, c):
    if len(refs) == 1:
        return refs[0][0]
    a, b = refs[0][0], refs[1][0]
    return jnp.concatenate([jnp.where(c == 0, a, b), jnp.where(c == 0, b, a)], axis=0)


def convolved(scratch, rim, body, taps_ref, bias_ref):
    rows = body.shape[0]
    taps = taps_ref.shape[0]
    scratch[0:8] = rim
    scratch[8 : 8 + rows] = body
    total = bias_ref[...]
    for k in range(taps):
        start = 8 - (taps - 1) + k
        total = total + taps_ref[k : k + 1] * scratch[start : start + rows]
    return silu(total)


def front_kernel(per, hd, sc, *refs):
    x_refs, refs = refs[:per], refs[per:]
    bc_refs, refs = refs[:per], refs[per:]
    (rim_x, rim_bc, dt, col, cx, cbc, bx, bbc, start) = refs[:9]
    (act_o, bc_o, run_o, step_o, pack_o, own_o, dec_o, start_o) = refs[9:17]
    xs, bs, bt = refs[17:]
    s, half = pl.program_id(0), pl.program_id(1)
    c, u = sc[0], sc[1]
    heads, rows = dt.shape[1:]
    n = bt.shape[0]
    bw = act_o.shape[2]

    @pl.when(half == 0)
    def _():
        at = u * rows + lax.broadcasted_iota(jnp.int32, (heads, rows), 1)
        live = jnp.where(at < sc[2 + s], 1.0, 0.0)
        step = softplus(dt[0] + col[:, 1:2]) * live
        i = lax.broadcasted_iota(jnp.int32, (rows, rows), 0)
        j = lax.broadcasted_iota(jnp.int32, (rows, rows), 1)
        run = exact(-col[:, 0:1] * step, (i <= j).astype(f32))
        to_end = jnp.exp(run[:, rows - 1 :] - run) * step
        run_o[0] = run
        step_o[0] = step
        pack_o[0] = jnp.transpose(jnp.concatenate([to_end, jnp.exp(run), run, step], axis=0))
        bc = convolved(bs, rim_bc[0], joined(bc_refs, c).astype(f32), cbc, bbc)
        bc_o[0] = bc
        bt[...] = jnp.transpose(bc[:, :n])

    act = convolved(xs, rim_x[0], joined(x_refs, c).astype(f32), cx, bx)
    act_o[0] = act
    first = half * (bw // hd)
    weighted = act * exact(pack_o[0], to_channels(bw, hd, first))
    own = exact(bt[...], weighted)
    decay = exact(pack_o[0, rows - 8 :, :], to_channels(bw, hd, first + heads))[7:8]
    dec_o[0] = jnp.broadcast_to(decay, (8, bw))

    @pl.when(u == 0)
    def _():
        begin = jnp.transpose(start[0])
        own_o[0] = own + decay * begin
        start_o[0] = begin.astype(bf16)

    @pl.when(u != 0)
    def _():
        own_o[0] = own
        start_o[0] = jnp.zeros(start_o.shape[1:], bf16)


def local_kernel(hd, act, bc, run, step, pack, skip, y_o, scores):
    half = pl.program_id(1)
    heads, rows = run.shape[1:]
    bw = act.shape[2]
    n = bc.shape[2] // 2

    @pl.when(half == 0)
    def _():
        scores[...] = exact_t(bc[0, :, n:], bc[0, :, :n])

    i = lax.broadcasted_iota(jnp.int32, (rows, rows), 0)
    j = lax.broadcasted_iota(jnp.int32, (rows, rows), 1)
    lower = i >= j
    lane = lax.broadcasted_iota(jnp.int32, (rows, lanes), 1)
    each = lanes // hd
    first = half * (bw // hd)

    def block(q, carry):
        at = pl.ds(pl.multiple_of(q * lanes, lanes), lanes)
        x = act[0, :, at]
        x_hi, x_lo = halves(x)
        y = skip[:, at] * x
        for e in range(each):
            h = first + q * each + e
            column = jnp.sum(jnp.where(lane == h + 2 * heads, pack[0], 0.0), axis=1, keepdims=True)
            gap = column - run[0, pl.ds(h, 1), :]
            mixing = jnp.exp(jnp.where(lower, gap, -1e30)) * (scores[...] * step[0, pl.ds(h, 1), :])
            m_hi, m_lo = halves(mixing)
            got = one_pass(m_hi, x_hi) + (one_pass(m_lo, x_hi) + one_pass(m_hi, x_lo))
            y = y + jnp.where(lane // hd == e, got, 0.0)
        y_o[0, :, at] = y
        return carry

    lax.fori_loop(0, bw // lanes, block, 0)


def back_kernel(per, hd, heads, sc, *refs):
    g_refs, refs = refs[:per], refs[per:]
    entry, bc, pack, local, gain, out_o, mixed = refs
    token_block = pl.program_id(0)
    c = sc[0]
    parts, n, bw = entry.shape
    gate = g_refs[0][0]
    if per == 2:
        gate = jnp.where(token_block == c, gate, g_refs[1][0])
    c_hi, c_lo = halves(bc[0, :, n:])
    total = None
    for k in range(parts):
        at = slice(k * bw, (k + 1) * bw)
        seen = one_pass(c_hi, entry[k]) + one_pass(c_lo, entry[k])
        grow = exact(pack[0], to_channels(bw, hd, heads + k * (bw // hd)))
        y = local[0, :, at] + grow * seen
        v = y * silu(gate[:, at].astype(f32))
        mixed[:, at] = v
        square = jnp.sum(v * v, axis=1, keepdims=True)
        total = square if total is None else total + square
    scale = lax.rsqrt(total / (parts * bw) + epsilon)
    out_o[0] = (mixed[...] * scale * gain[...]).astype(bf16)


def window_kernel(hd, full, factor, taps_ref, bias_ref, skip, local_o, c_o):
    taps = taps_ref.shape[0]
    steps, rows, gwidth = local_o.shape
    n = c_o.shape[2]
    acts = []
    for i in range(steps):
        total = bias_ref[...]
        for k in range(taps):
            total = total + taps_ref[k : k + 1] * full[i + k]
        acts.append(silu(total))
    coef = []
    for i in range(steps):
        read = acts[i][:, gwidth + n :]
        c_o[i] = read
        for j in range(i + 1):
            both = jnp.sum(read * acts[j][:, gwidth : gwidth + n], axis=1, keepdims=True)
            coef.append(both * factor[len(coef)])
    wide = exact(jnp.concatenate(coef, axis=0), to_channels(gwidth, hd, 0))
    at = 0
    for i in range(steps):
        y = skip[...] * acts[i][:, :gwidth]
        for j in range(i + 1):
            y = y + wide[at * rows : (at + 1) * rows] * acts[j][:, :gwidth]
            at += 1
        local_o[i] = y


def read_kernel(hd, asked, own, after, out_o):
    half = pl.program_id(0)
    prompts, _, n, bw = own.shape
    spread = exact(jnp.exp(after[...]), to_channels(bw, hd, half * (bw // hd)))
    rows = asked[:, :n]
    prompt = asked[:, n : n + 1]
    total = None
    for s in range(prompts):
        c_hi, c_lo = halves(jnp.where(prompt == s, rows, 0.0))
        s_hi, s_lo = halves(own[s, 0] * spread[s : s + 1])
        got = one_pass(c_hi, s_hi) + (one_pass(c_lo, s_hi) + one_pass(c_hi, s_lo))
        total = got if total is None else total + got
    out_o[...] = total.astype(bf16)


def finish_kernel(hd, *refs):
    *sums, local, grow, gate, gain, out_o = refs
    total = sums[0][...].astype(f32)
    for r in sums[1:]:
        total = total + r[...].astype(f32)
    gwidth = out_o.shape[1]
    y = exact(grow[...], to_channels(gwidth, hd, 0)) * total + local[...]
    v = y * silu(gate[...])
    scale = lax.rsqrt(jnp.mean(v * v, axis=1, keepdims=True) + epsilon)
    out_o[...] = (v * scale * gain[...]).astype(bf16)


def params():
    return pltpu.CompilerParams(vmem_limit_bytes=vmem)


def shards(
    inner_x,
    gate_z,
    proj_bc,
    dt_raw,
    a_log,
    dt_bias,
    d_skip,
    conv_x,
    conv_bc,
    bias_x,
    bias_bc,
    norm_gain,
    init_state,
    init_conv_x,
    init_conv_bc,
    lengths,
    dec_x,
    dec_z,
    dec_bc,
    dec_dt,
    row_prompt,
    w_out,
):
    prompts, tokens, width = inner_x.shape
    groups, pair = proj_bc.shape[2:]
    ns = pair // 2
    heads = dt_raw.shape[1] // groups
    gwidth = width // groups
    hd = gwidth // heads
    taps = conv_x.shape[0]
    steps, batch = dec_x.shape[:2]
    cols = w_out.shape[1]
    n = lax.axis_size("ctx")
    tp = lax.axis_size("tp")
    assert groups in (1, 2) and n % groups == 0 and 4 * heads == lanes
    per = groups
    m = n // per
    device = lax.axis_index("ctx")
    u, c = device // per, device % per
    unit_tokens = per * tokens
    rows_u = per * batch
    per_prompt = 2
    bw = gwidth // per_prompt
    parts = prompts * per_prompt

    def mine(arr, axis):
        return lax.dynamic_index_in_dim(arr, c, axis, keepdims=False)

    def swap(arr):
        return lax.ppermute(arr, "ctx", [(i, i ^ 1) for i in range(n)])

    def in_order(own, other, axis):
        first = jnp.where(c == 0, own, other)
        second = jnp.where(c == 0, other, own)
        return jnp.concatenate([first, second], axis=axis)

    def other_group(arr, size):
        if per == 1:
            return None
        at = [0] * (arr.ndim - 1) + [(1 - c) * size]
        return swap(lax.dynamic_slice(arr, at, arr.shape[:-1] + (size,)))

    def pair_up(arr, gaxis, taxis):
        if per == 1:
            return jnp.squeeze(arr, gaxis)
        other = swap(lax.dynamic_index_in_dim(arr, 1 - c, gaxis, keepdims=False))
        return in_order(mine(arr, gaxis), other, taxis)

    def shift(arr, k):
        return lax.ppermute(arr, "ctx", [(i, (i + k * per) % n) for i in range(n)])

    bc_flat = proj_bc.reshape(prompts, tokens, groups * pair)
    x_other = other_group(inner_x, gwidth)
    bc_other = other_group(bc_flat, pair)
    last_x = inner_x[:, tokens - taps + 1 :]
    last_bc = bc_flat[:, tokens - taps + 1 :]
    wide = gwidth + pair
    rim = jnp.zeros((prompts, taps - 1, wide), bf16)
    for g in range(per):
        pairs = [(v * per + per - 1, (v + 1) * per + g) for v in range(m - 1)]
        send = jnp.concatenate(
            [last_x[..., g * gwidth : (g + 1) * gwidth], last_bc[..., g * pair : (g + 1) * pair]],
            axis=-1,
        )
        got = lax.ppermute(send, "ctx", pairs)
        rim = jnp.where(c == g, got, rim)
    places = device * tokens + jnp.arange(tokens, dtype=jnp.int32)
    target = lengths[:, None] - (taps - 1) + jnp.arange(taps - 1, dtype=jnp.int32)[None, :]
    picker = (places[None, None, :] == target[:, :, None]).astype(bf16)
    tails = jnp.concatenate(
        [
            jnp.einsum("sjt,stc->sjc", picker, inner_x, preferred_element_type=f32),
            jnp.einsum("sjt,stc->sjc", picker, bc_flat, preferred_element_type=f32),
        ],
        axis=-1,
    )
    tails = lax.psum(tails, "ctx")
    dt = pair_up(dt_raw.reshape(prompts, groups, heads, tokens), 1, 2)
    z_other = other_group(gate_z, gwidth)
    dec_bc_flat = dec_bc.reshape(steps, batch, groups * pair)
    dec_flat = jnp.concatenate(
        [
            jnp.concatenate(
                [dec_x[..., g * gwidth : (g + 1) * gwidth], dec_bc_flat[..., g * pair : (g + 1) * pair],
                 dec_z[..., g * gwidth : (g + 1) * gwidth]],
                axis=-1,
            )[:, :, None]
            for g in range(groups)
        ],
        axis=2,
    )
    dec_all = pair_up(dec_flat, 2, 1).astype(f32)
    dec_raw, dec_gate = dec_all[..., :wide], dec_all[..., wide:]
    dec_step = pair_up(dec_dt.reshape(steps, groups, heads, batch), 1, 2)
    prompt_of = row_prompt if per == 1 else in_order(row_prompt, swap(row_prompt), 0)

    rate = jnp.exp(mine(a_log.reshape(groups, heads), 0))
    dtb = mine(dt_bias.reshape(groups, heads), 0)
    skip = jnp.repeat(mine(d_skip.reshape(groups, heads), 0), hd)[None]
    gain = mine(norm_gain.reshape(groups, 1, gwidth), 0)
    col = jnp.pad(jnp.stack([rate, dtb], axis=1), ((0, 0), (0, lanes - 2)))
    cbc = conv_bc.reshape(taps, groups * pair)
    bbc = bias_bc.reshape(1, groups * pair)
    bx = bias_x.reshape(1, width)
    start_rim = jnp.concatenate(
        [
            mine(init_conv_x.reshape(prompts, taps - 1, groups, gwidth), 2),
            mine(init_conv_bc, 2),
        ],
        axis=-1,
    )
    rim = jnp.where(u == 0, start_rim, rim).astype(f32)
    rim = jnp.pad(rim, ((0, 0), (8 - (taps - 1), 0), (0, 0)))
    start = init_state.reshape(prompts, groups * gwidth, ns)
    sc = jnp.concatenate([jnp.stack([c, u]).astype(jnp.int32), lengths])

    x_in = [inner_x] + ([x_other] if per == 2 else [])
    bc_in = [bc_flat] + ([bc_other] if per == 2 else [])
    T = unit_tokens
    spec = pl.BlockSpec
    in_specs = [spec((1, tokens, bw), lambda s, k, sc: (s, 0, sc[0] * per_prompt + k))]
    in_specs += [spec((1, tokens, bw), lambda s, k, sc: (s, 0, k))] * (per - 1)
    in_specs += [spec((1, tokens, pair), lambda s, k, sc: (s, 0, sc[0]))]
    in_specs += [spec((1, tokens, pair), lambda s, k, sc: (s, 0, 0))] * (per - 1)
    in_specs += [
        spec((1, 8, bw), lambda s, k, sc: (s, 0, k)),
        spec((1, 8, pair), lambda s, k, sc: (s, 0, 0)),
        spec((1, heads, T), lambda s, k, sc: (s, 0, 0)),
        spec((heads, lanes), lambda s, k, sc: (0, 0)),
        spec((taps, bw), lambda s, k, sc: (0, sc[0] * per_prompt + k)),
        spec((taps, pair), lambda s, k, sc: (0, sc[0])),
        spec((1, bw), lambda s, k, sc: (0, sc[0] * per_prompt + k)),
        spec((1, pair), lambda s, k, sc: (0, sc[0])),
        spec((1, bw, ns), lambda s, k, sc: (s, sc[0] * per_prompt + k, 0)),
    ]
    chunk = lambda s, k, sc: (s * per_prompt + k, 0, 0)
    whole = lambda s, k, sc: (s, 0, 0)
    act, bc, run, step, pack, own, decay, begin = pl.pallas_call(
        functools.partial(front_kernel, per, hd),
        grid_spec=pltpu.PrefetchScalarGridSpec(
            num_scalar_prefetch=1,
            grid=(prompts, per_prompt),
            in_specs=in_specs,
            out_specs=[
                spec((1, T, bw), lambda s, k, sc: (s, 0, k)),
                spec((1, T, pair), whole),
                spec((1, heads, T), whole),
                spec((1, heads, T), whole),
                spec((1, T, lanes), whole),
                spec((1, ns, bw), chunk),
                spec((1, 8, bw), chunk),
                spec((1, ns, bw), chunk),
            ],
            scratch_shapes=[
                pltpu.VMEM((T + 8, bw), f32),
                pltpu.VMEM((T + 8, pair), f32),
                pltpu.VMEM((ns, T), f32),
            ],
        ),
        out_shape=[
            jax.ShapeDtypeStruct((prompts, T, gwidth), f32),
            jax.ShapeDtypeStruct((prompts, T, pair), f32),
            jax.ShapeDtypeStruct((prompts, heads, T), f32),
            jax.ShapeDtypeStruct((prompts, heads, T), f32),
            jax.ShapeDtypeStruct((prompts, T, lanes), f32),
            jax.ShapeDtypeStruct((parts, ns, bw), f32),
            jax.ShapeDtypeStruct((parts, 8, bw), f32),
            jax.ShapeDtypeStruct((parts, ns, bw), bf16),
        ],
        compiler_params=params(),
        name="front",
    )(sc, *x_in, *bc_in, rim[..., :gwidth], rim[..., gwidth:], dt, col, conv_x, cbc, bx, bbc, start)

    arrived = []
    carry = jnp.zeros(own.shape[1:], bf16)
    along = [(i, i + per) for i in range(n - per)]
    for t in range(parts + m - 2):
        at_k = jnp.clip(t - u, 0, parts - 1)
        own_t = lax.dynamic_index_in_dim(own, at_k, 0, keepdims=False)
        decay_t = lax.dynamic_index_in_dim(decay, at_k, 0, keepdims=False)[:1]
        leave = (decay_t * carry.astype(f32) + own_t).astype(bf16)
        carry = lax.ppermute(leave, "ctx", along)
        arrived.append(carry)

    y_local = pl.pallas_call(
        functools.partial(local_kernel, hd),
        grid=(prompts, per_prompt),
        in_specs=[
            spec((1, T, bw), lambda s, k: (s, 0, k)),
            spec((1, T, pair), lambda s, k: (s, 0, 0)),
            spec((1, heads, T), lambda s, k: (s, 0, 0)),
            spec((1, heads, T), lambda s, k: (s, 0, 0)),
            spec((1, T, lanes), lambda s, k: (s, 0, 0)),
            spec((1, bw), lambda s, k: (0, k)),
        ],
        out_specs=spec((1, T, bw), lambda s, k: (s, 0, k)),
        out_shape=jax.ShapeDtypeStruct((prompts, T, gwidth), f32),
        scratch_shapes=[pltpu.VMEM((T, T), f32)],
        compiler_params=params(),
        cost_estimate=pl.CostEstimate(
            flops=60_000 * T * T, bytes_accessed=16 * T * gwidth, transcendentals=0
        ),
        name="local",
    )(act, bc, run, step, pack, skip)

    tails_g = jnp.concatenate(
        [
            lax.dynamic_slice_in_dim(tails, c * gwidth, gwidth, 2),
            lax.dynamic_slice_in_dim(tails, width + c * pair, pair, 2),
        ],
        axis=-1,
    )
    window = tails_g[0][:, None]
    for s in range(1, prompts):
        window = jnp.where(prompt_of[None, :, None] == s, tails_g[s][:, None], window)
    window = jnp.broadcast_to(window, (taps - 1, rows_u, wide))
    full = jnp.concatenate([window, dec_raw], axis=0)
    tap_w = jnp.concatenate(
        [mine(conv_x.reshape(taps, groups, gwidth), 1), mine(conv_bc, 1)], axis=-1
    )
    tap_b = jnp.concatenate([mine(bias_x.reshape(groups, gwidth), 0), mine(bias_bc, 0)])[None]
    stepd = jax.nn.softplus(jnp.transpose(dec_step, (0, 2, 1)) + dtb)
    logd = -rate * stepd
    upto = [logd[0]]
    for i in range(1, steps):
        upto.append(upto[-1] + logd[i])
    factor = jnp.stack(
        [jnp.exp(upto[i] - upto[j]) * stepd[j] for i in range(steps) for j in range(i + 1)]
    )
    factor = jnp.pad(factor, ((0, 0), (0, 0), (0, lanes - heads)))
    grow = jnp.pad(
        jnp.exp(jnp.stack(upto)).reshape(steps * rows_u, heads), ((0, 0), (0, lanes - heads))
    )
    local, cd = pl.pallas_call(
        functools.partial(window_kernel, hd),
        out_shape=[
            jax.ShapeDtypeStruct((steps, rows_u, gwidth), f32),
            jax.ShapeDtypeStruct((steps, rows_u, ns), f32),
        ],
        compiler_params=params(),
        name="window",
    )(full, factor, tap_w, tap_b, skip)

    span = run[:, :, T - 1]
    asked_rows = steps * rows_u
    payload = jnp.concatenate(
        [
            jnp.concatenate(
                [
                    cd.reshape(asked_rows, ns),
                    jnp.broadcast_to(
                        jnp.tile(prompt_of.astype(f32), steps)[:, None], (asked_rows, lanes)
                    ),
                ],
                axis=1,
            ),
            jnp.pad(span, ((0, 8 - prompts), (0, ns + lanes - heads))),
        ],
        axis=0,
    )
    blocks = [payload] + [shift(payload, k) for k in range(1, m)]
    after = jnp.zeros((8, lanes), f32)
    for k in range(1, m):
        span_k = blocks[k][asked_rows:, :lanes]
        after = after + jnp.where((u - k) % m > u, span_k, 0.0)
    asked = jnp.concatenate([b[:asked_rows] for b in blocks], axis=0)
    read = pl.pallas_call(
        functools.partial(read_kernel, hd),
        grid=(per_prompt,),
        in_specs=[
            spec((m * asked_rows, ns + lanes), lambda k: (0, 0)),
            spec((prompts, 1, ns, bw), lambda k: (0, k, 0, 0)),
            spec((8, lanes), lambda k: (0, 0)),
        ],
        out_specs=spec((m * asked_rows, bw), lambda k: (0, k)),
        out_shape=jax.ShapeDtypeStruct((m * asked_rows, gwidth), bf16),
        compiler_params=params(),
        name="read",
    )(asked, own.reshape(prompts, per_prompt, ns, bw), after)
    sums = [read[:asked_rows]]
    for k in range(1, m):
        sums.append(shift(read[k * asked_rows : (k + 1) * asked_rows], -k))
    hidden = pl.pallas_call(
        functools.partial(finish_kernel, hd),
        out_shape=jax.ShapeDtypeStruct((asked_rows, gwidth), bf16),
        compiler_params=params(),
        name="finish",
    )(*sums, local.reshape(asked_rows, gwidth), grow, dec_gate.reshape(asked_rows, gwidth), gain)
    hidden = hidden.reshape(steps, rows_u, gwidth)
    got = jnp.stack([hidden] + [shift(hidden, k) for k in range(1, m)])
    got = jnp.concatenate([got[::-1], got[::-1]])
    got = lax.dynamic_slice_in_dim(got, m - 1 - u, m, 0)
    if per == 2:
        got = in_order(got, swap(got), 3)
    product = jnp.dot(
        jnp.swapaxes(got, 0, 1).reshape(-1, width), w_out, preferred_element_type=f32
    )
    terms = lax.all_to_all(product.reshape(steps, tp, -1, cols), "tp", 1, 1)
    layer_out = jnp.sum(terms, axis=1).astype(bf16)

    outs = []
    for s in range(prompts):
        entry = []
        for k in range(s * per_prompt, (s + 1) * per_prompt):
            e = begin[k]
            for v in range(1, m):
                e = jnp.where(u == v, arrived[k + v - 1], e)
            entry.append(e)
        z_in = [gate_z] + ([z_other] if per == 2 else [])
        z_specs = [spec((1, tokens, gwidth), lambda j, sc, s=s: (s, 0, sc[0]))]
        z_specs += [spec((1, tokens, gwidth), lambda j, sc, s=s: (s, 0, 0))] * (per - 1)
        out = pl.pallas_call(
            functools.partial(back_kernel, per, hd, heads),
            grid_spec=pltpu.PrefetchScalarGridSpec(
                num_scalar_prefetch=1,
                grid=(per,),
                in_specs=z_specs
                + [
                    spec((per_prompt, ns, bw), lambda j, sc: (0, 0, 0)),
                    spec((1, tokens, pair), lambda j, sc, s=s: (s, j, 0)),
                    spec((1, tokens, lanes), lambda j, sc, s=s: (s, j, 0)),
                    spec((1, tokens, gwidth), lambda j, sc, s=s: (s, j, 0)),
                    spec((1, gwidth), lambda j, sc: (0, 0)),
                ],
                out_specs=spec(
                    (1, tokens, gwidth), lambda j, sc: (jnp.where(j == sc[0], 0, 1), 0, 0)
                ),
                scratch_shapes=[pltpu.VMEM((tokens, gwidth), f32)],
            ),
            out_shape=jax.ShapeDtypeStruct((per, tokens, gwidth), bf16),
            compiler_params=params(),
            name="back",
        )(sc, *z_in, jnp.stack(entry), bc, pack, y_local, gain)
        outs.append(out[0] if per == 1 else in_order(out[0], swap(out[1]), 1))
    return (jnp.stack(outs), layer_out)


def solution(mesh):
    in_specs = (
        P(None, "ctx", "tp"),
        P(None, "ctx", "tp"),
        P(None, "ctx", "tp", None),
        P(None, "tp", "ctx"),
        P("tp"),
        P("tp"),
        P("tp"),
        P(None, "tp"),
        P(None, "tp", None),
        P("tp"),
        P("tp", None),
        P("tp"),
        P(None, "tp", None, None),
        P(None, None, "tp"),
        P(None, None, "tp", None),
        P(),
        P(None, "ctx", "tp"),
        P(None, "ctx", "tp"),
        P(None, "ctx", "tp", None),
        P(None, "tp", "ctx"),
        P("ctx"),
        P("tp", "ctx"),
    )
    out_specs = (P(None, "ctx", "tp"), P(None, "tp", "ctx"))
    return jax.shard_map(shards, mesh=mesh, in_specs=in_specs, out_specs=out_specs, check_vma=False)
```

```python
import functools

import jax
import jax.numpy as jnp
from jax import lax
from jax.experimental import pallas as pl
from jax.experimental.pallas import tpu as pltpu
from jax.sharding import PartitionSpec as P

epsilon = 1e-05
highest = lax.Precision.HIGHEST
f32, bf16 = jnp.float32, jnp.bfloat16
lanes = 128
vmem = 40 * 1024 * 1024


def silu(v):
    return v * (1.0 / (1.0 + jnp.exp(-v)))


def softplus(v):
    return jnp.maximum(v, 0.0) + jnp.log1p(jnp.exp(-jnp.abs(v)))


def exact(a, b):
    return jnp.dot(a, b, precision=highest, preferred_element_type=f32)


def exact_t(a, b):
    return lax.dot_general(
        a, b, (((1,), (1,)), ((), ())), precision=highest, preferred_element_type=f32
    )


def one_pass(a, b):
    return jnp.dot(a, b, preferred_element_type=f32)


def halves(a):
    high = a.astype(bf16)
    return high, (a - high.astype(f32)).astype(bf16)


def to_channels(columns, hd, first):
    row = lax.broadcasted_iota(jnp.int32, (lanes, columns), 0)
    col = lax.broadcasted_iota(jnp.int32, (lanes, columns), 1)
    return (row == col // hd + first).astype(f32)


def joined(refs, c, axis=0):
    if len(refs) == 1:
        return refs[0][0]
    a, b = refs[0][0], refs[1][0]
    return jnp.concatenate([jnp.where(c == 0, a, b), jnp.where(c == 0, b, a)], axis=axis)


def convolved(scratch, rim, body, taps_ref, bias_ref):
    rows = body.shape[0]
    taps = taps_ref.shape[0]
    scratch[0:8] = rim
    scratch[8 : 8 + rows] = body
    total = bias_ref[...]
    for k in range(taps):
        start = 8 - (taps - 1) + k
        total = total + taps_ref[k : k + 1] * scratch[start : start + rows]
    return silu(total)


def front_kernel(per, hd, prompt, sc, *refs):
    x_refs, refs = refs[:per], refs[per:]
    bc_refs, refs = refs[:per], refs[per:]
    dt_refs, refs = refs[:per], refs[per:]
    (rim_x, rim_bc, col, cx, cbc, bx, bbc, start) = refs[:8]
    (act_o, bc_o, run_o, step_o, pack_o, own_o, dec_o, start_o) = refs[8:16]
    xs, bs, bt = refs[16:]
    half = pl.program_id(0)
    c, u = sc[0], sc[1]
    _, heads, rows = run_o.shape
    n = bt.shape[0]
    bw = act_o.shape[2]

    @pl.when(half == 0)
    def _():
        at = u * rows + lax.broadcasted_iota(jnp.int32, (heads, rows), 1)
        live = jnp.where(at < sc[2 + prompt], 1.0, 0.0)
        step = softplus(joined(dt_refs, c, 1) + col[:, 1:2]) * live
        i = lax.broadcasted_iota(jnp.int32, (rows, rows), 0)
        j = lax.broadcasted_iota(jnp.int32, (rows, rows), 1)
        run = exact(-col[:, 0:1] * step, (i <= j).astype(f32))
        to_end = jnp.exp(run[:, rows - 1 :] - run) * step
        run_o[0] = run
        step_o[0] = step
        pack_o[0] = jnp.transpose(jnp.concatenate([to_end, jnp.exp(run), run, step], axis=0))
        bc = convolved(bs, rim_bc[0], joined(bc_refs, c).astype(f32), cbc, bbc)
        bc_o[0] = bc
        bt[...] = jnp.transpose(bc[:, :n])

    act = convolved(xs, rim_x[0], joined(x_refs, c).astype(f32), cx, bx)
    act_o[0] = act
    first = half * (bw // hd)
    weighted = act * exact(pack_o[0], to_channels(bw, hd, first))
    own = exact(bt[...], weighted)
    decay = exact(pack_o[0, rows - 8 :, :], to_channels(bw, hd, first + heads))[7:8]
    dec_o[0] = jnp.broadcast_to(decay, (8, bw))

    @pl.when(u == 0)
    def _():
        begin = jnp.transpose(start[0])
        own_o[0] = own + decay * begin
        start_o[0] = begin.astype(bf16)

    @pl.when(u != 0)
    def _():
        own_o[0] = own
        start_o[0] = jnp.zeros(start_o.shape[1:], bf16)


def local_kernel(hd, at_part, act, bc, run, step, pack, skip, y_o, scores):
    half = pl.program_id(0) + at_part
    heads, rows = run.shape[1:]
    bw = act.shape[2]
    n = bc.shape[2] // 2

    scores[...] = exact_t(bc[0, :, n:], bc[0, :, :n])

    i = lax.broadcasted_iota(jnp.int32, (rows, rows), 0)
    j = lax.broadcasted_iota(jnp.int32, (rows, rows), 1)
    lower = i >= j
    lane = lax.broadcasted_iota(jnp.int32, (rows, lanes), 1)
    each = lanes // hd
    first = half * (bw // hd)

    def block(q, carry):
        at = pl.ds(pl.multiple_of(q * lanes, lanes), lanes)
        x = act[0, :, at]
        x_hi, x_lo = halves(x)
        y = skip[:, at] * x
        for e in range(each):
            h = first + q * each + e
            column = jnp.sum(jnp.where(lane == h + 2 * heads, pack[0], 0.0), axis=1, keepdims=True)
            gap = column - run[0, pl.ds(h, 1), :]
            mixing = jnp.exp(jnp.where(lower, gap, -1e30)) * (scores[...] * step[0, pl.ds(h, 1), :])
            m_hi, m_lo = halves(mixing)
            got = one_pass(m_hi, x_hi) + (one_pass(m_lo, x_hi) + one_pass(m_hi, x_lo))
            y = y + jnp.where(lane // hd == e, got, 0.0)
        y_o[0, :, at] = y
        return carry

    lax.fori_loop(0, bw // lanes, block, 0)


def back_kernel(per, hd, heads, sc, *refs):
    g_refs, refs = refs[:per], refs[per:]
    *rest, out_o, mixed = refs
    parts = (len(rest) - 3) // 2
    entry, (bc, pack, gain), local = rest[:parts], rest[parts : parts + 3], rest[parts + 3 :]
    token_block = pl.program_id(0)
    c = sc[0]
    _, n, bw = entry[0].shape
    gate = g_refs[0][0]
    if per == 2:
        gate = jnp.where(token_block == c, gate, g_refs[1][0])
    c_hi, c_lo = halves(bc[0, :, n:])
    total = None
    for k in range(parts):
        at = slice(k * bw, (k + 1) * bw)
        seen = one_pass(c_hi, entry[k][0]) + one_pass(c_lo, entry[k][0])
        grow = exact(pack[0], to_channels(bw, hd, heads + k * (bw // hd)))
        y = local[k][0] + grow * seen
        v = y * silu(gate[:, at].astype(f32))
        mixed[:, at] = v
        square = jnp.sum(v * v, axis=1, keepdims=True)
        total = square if total is None else total + square
    scale = lax.rsqrt(total / (parts * bw) + epsilon)
    out_o[0] = (mixed[...] * scale * gain[...]).astype(bf16)


def rows_of(refs, i, at, c):
    a = refs[0][i][:, at[0]].astype(f32)
    if len(refs) == 1:
        return a
    b = refs[1][i][:, at[1]].astype(f32)
    return jnp.concatenate([jnp.where(c == 0, a, b), jnp.where(c == 0, b, a)], axis=0)


def window_kernel(per, hd, heads, sc, *refs):
    x_ref, bc_ref, refs = refs[0], refs[1], refs[2:]
    other, refs = refs[: per - 1], refs[per - 1 :]
    small, refs = refs[:per], refs[per:]
    *tails, last0, last1, par, cx, cbc, bx, bbc, local_o, grow_o, pay_o = refs
    c = sc[0]
    taps = cx.shape[0]
    steps, batch, gwidth = x_ref.shape
    pair = bc_ref.shape[2]
    ns = pair // 2
    rows = per * batch
    whole = slice(None)
    tail = sum(t[...].astype(f32) for t in tails)
    prompt = rows_of(small, steps, (whole, whole), c)
    body_x = [rows_of([x_ref, *other], i, (whole, slice(0, gwidth)), c) for i in range(steps)]
    body_bc = [
        rows_of([bc_ref, *other], i, (whole, slice(gwidth, gwidth + pair)), c) for i in range(steps)
    ]

    def window(lo, hi, body):
        out = []
        for j in range(taps - 1):
            first, second = tail[j : j + 1, lo:hi], tail[8 + j : 9 + j, lo:hi]
            out.append(jnp.where(prompt[:, :1] == 0.0, first, second))
        return out + body

    def conv(full, taps_ref, bias):
        acts = []
        for i in range(steps):
            total = bias
            for k in range(taps):
                total = total + taps_ref[k : k + 1] * full[i + k]
            acts.append(silu(total))
        return acts

    xd = conv(window(0, gwidth, body_x), cx, bx[...])
    mix = conv(window(gwidth, gwidth + pair, body_bc), cbc, bbc[...])
    rate, dtb, skip = par[0:1], par[1:2], par[2:3]
    step = [softplus(rows_of(small, i, (whole, whole), c) + dtb) for i in range(steps)]
    upto = []
    for i in range(steps):
        upto.append((upto[-1] if upto else 0.0) - rate * step[i])
    coef = [jnp.broadcast_to(skip, (8, lanes))]
    for i in range(steps):
        read = mix[i][:, ns:]
        pay_o[i * rows : (i + 1) * rows, :ns] = read
        pay_o[i * rows : (i + 1) * rows, ns:] = prompt
        grow_o[i * rows : (i + 1) * rows] = jnp.exp(upto[i])
        for j in range(i + 1):
            both = jnp.sum(read * mix[j][:, :ns], axis=1, keepdims=True)
            coef.append(both * (jnp.exp(upto[i] - upto[j]) * step[j]))
    wide = exact(jnp.concatenate(coef, axis=0), to_channels(gwidth, hd, c * heads))
    at = 8
    for i in range(steps):
        y = wide[0:1] * xd[i]
        for j in range(i + 1):
            y = y + wide[at : at + rows] * xd[j]
            at += rows
        local_o[i * rows : (i + 1) * rows] = y
    pay_o[steps * rows :, :ns] = jnp.zeros((8, ns), f32)
    pay_o[steps * rows :, ns:] = jnp.concatenate(
        [last0[0, 7:8], last1[0, 7:8], jnp.zeros((6, lanes), f32)], axis=0
    )


def read_kernel(hd, heads, m, sc, *refs):
    blocks, own, outs = refs[:m], refs[m:-m], refs[-m:]
    half = pl.program_id(0)
    _, ns, bw = own[0].shape
    u = sc[1]
    rows = blocks[0].shape[0] - 8
    after = jnp.zeros((8, lanes), f32)
    for k in range(1, m):
        after = after + jnp.where(k > u, blocks[k][rows:, ns:], 0.0)
    spread = exact(jnp.exp(after), to_channels(bw, hd, 2 * heads + half * (bw // hd)))
    asked = jnp.concatenate([b[:rows, :ns] for b in blocks], axis=0)
    prompt = jnp.concatenate([b[:rows, ns : ns + 1] for b in blocks], axis=0)
    total = None
    for s in range(len(own)):
        c_hi, c_lo = halves(jnp.where(prompt == s, asked, 0.0))
        s_hi, s_lo = halves(own[s][0] * spread[s : s + 1])
        got = one_pass(c_hi, s_hi) + (one_pass(c_lo, s_hi) + one_pass(c_hi, s_lo))
        total = got if total is None else total + got
    for k in range(m):
        outs[k][...] = total[k * rows : (k + 1) * rows].astype(bf16)


def finish_kernel(per, hd, heads, m, sc, *refs):
    sums, local, grow, z_ref, refs = refs[:m], refs[m], refs[m + 1], refs[m + 2], refs[m + 3 :]
    *other, gain, out_o = refs
    c = sc[0]
    steps = z_ref.shape[0]
    gwidth = out_o.shape[1]
    total = sums[0][...].astype(f32)
    for r in sums[1:]:
        total = total + r[...].astype(f32)
    y = exact(grow[...], to_channels(gwidth, hd, c * heads)) * total + local[...]
    at = (slice(None), slice(other[0].shape[2] - gwidth, None) if other else None)
    gate = jnp.concatenate([rows_of([z_ref, *other], i, at, c) for i in range(steps)], axis=0)
    v = y * silu(gate)
    scale = lax.rsqrt(jnp.mean(v * v, axis=1, keepdims=True) + epsilon)
    out_o[...] = (v * scale * gain[...]).astype(bf16)


def project_kernel(per, m, sc, *refs):
    mine, other, w, out_o = refs[:m], refs[m:-2], refs[-2], refs[-1]
    c, u = sc[0], sc[1]
    tp, steps, rows_tp, cols = out_o.shape
    a = jnp.concatenate([r[...] for r in mine], axis=0)
    gwidth = a.shape[1]
    if per == 2:
        b = jnp.concatenate([r[...] for r in other], axis=0)
        total = one_pass(jnp.where(c == 0, a, b), w[:gwidth])
        total = total + one_pass(jnp.where(c == 0, b, a), w[gwidth:])
    else:
        total = one_pass(a, w[...])
    rows = a.shape[0] // (m * steps)
    each = m // tp
    for k in range(m):
        v = lax.rem(u - k + m, m)
        at = pl.ds(pl.multiple_of(lax.rem(v, each) * rows, rows), rows)
        for i in range(steps):
            first = (k * steps + i) * rows
            out_o[v // each, i, at, :] = total[first : first + rows]


def params(limit=vmem):
    return pltpu.CompilerParams(vmem_limit_bytes=limit)


def cost(us):
    return pl.CostEstimate(flops=int(us * 1.1e9), bytes_accessed=int(us * 3e6), transcendentals=0)


def tied(first, then):
    return lax.optimization_barrier((first, then))


def shards(
    inner_x,
    gate_z,
    proj_bc,
    dt_raw,
    a_log,
    dt_bias,
    d_skip,
    conv_x,
    conv_bc,
    bias_x,
    bias_bc,
    norm_gain,
    init_state,
    init_conv_x,
    init_conv_bc,
    lengths,
    dec_x,
    dec_z,
    dec_bc,
    dec_dt,
    row_prompt,
    w_out,
):
    prompts, tokens, width = inner_x.shape
    groups, pair = proj_bc.shape[2:]
    ns = pair // 2
    heads = dt_raw.shape[1] // groups
    gwidth = width // groups
    hd = gwidth // heads
    taps = conv_x.shape[0]
    steps, batch = dec_x.shape[:2]
    cols = w_out.shape[1]
    n = lax.axis_size("ctx")
    tp = lax.axis_size("tp")
    assert groups in (1, 2) and n % groups == 0 and 4 * heads == lanes
    per = groups
    m = n // per
    device = lax.axis_index("ctx")
    u, c = device // per, device % per
    unit_tokens = per * tokens
    rows_u = per * batch
    per_prompt = 2
    bw = gwidth // per_prompt
    parts = prompts * per_prompt

    def mine(arr, axis):
        return lax.dynamic_index_in_dim(arr, c, axis, keepdims=False)

    def swap(arr):
        return lax.ppermute(arr, "ctx", [(i, i ^ 1) for i in range(n)])

    def in_order(own, other, axis):
        first = jnp.where(c == 0, own, other)
        second = jnp.where(c == 0, other, own)
        return jnp.concatenate([first, second], axis=axis)

    def other_group(arr, size):
        if per == 1:
            return None
        at = [0] * (arr.ndim - 1) + [(1 - c) * size]
        return swap(lax.dynamic_slice(arr, at, arr.shape[:-1] + (size,)))

    def pair_up(arr, gaxis, taxis):
        if per == 1:
            return jnp.squeeze(arr, gaxis)
        other = swap(lax.dynamic_index_in_dim(arr, 1 - c, gaxis, keepdims=False))
        return in_order(mine(arr, gaxis), other, taxis)

    def shift(arr, k):
        return lax.ppermute(arr, "ctx", [(i, (i + k * per) % n) for i in range(n)])

    bc_flat = proj_bc.reshape(prompts, tokens, groups * pair)
    x_other = bc_other = None
    if per == 2:
        x_send = lax.dynamic_slice_in_dim(inner_x, (1 - c) * gwidth, gwidth, 2)
        x_other = swap(x_send)
        bc_other = other_group(bc_flat, pair)
    last_x = inner_x[:, tokens - taps + 1 :]
    last_bc = bc_flat[:, tokens - taps + 1 :]
    wide = gwidth + pair
    rim = jnp.zeros((prompts, taps - 1, wide), bf16)
    for g in range(per):
        pairs = [(v * per + per - 1, (v + 1) * per + g) for v in range(m - 1)]
        send = jnp.concatenate(
            [last_x[..., g * gwidth : (g + 1) * gwidth], last_bc[..., g * pair : (g + 1) * pair]],
            axis=-1,
        )
        got = lax.ppermute(send, "ctx", pairs)
        rim = jnp.where(c == g, got, rim)
    dt_in = [dt_raw]
    if per == 2:
        given = lax.dynamic_slice_in_dim(dt_raw, (1 - c) * heads, heads, 1)
        dt_in.append(swap(given))

    rate = jnp.exp(mine(a_log.reshape(groups, heads), 0))
    dtb = mine(dt_bias.reshape(groups, heads), 0)
    skip = jnp.repeat(mine(d_skip.reshape(groups, heads), 0), hd)[None]
    gain = mine(norm_gain.reshape(groups, 1, gwidth), 0)
    col = jnp.pad(jnp.stack([rate, dtb], axis=1), ((0, 0), (0, lanes - 2)))
    cbc = conv_bc.reshape(taps, groups * pair)
    bbc = bias_bc.reshape(1, groups * pair)
    bx = bias_x.reshape(1, width)
    start_rim = jnp.concatenate(
        [
            mine(init_conv_x.reshape(prompts, taps - 1, groups, gwidth), 2),
            mine(init_conv_bc, 2),
        ],
        axis=-1,
    )
    rim = jnp.where(u == 0, start_rim, rim).astype(f32)
    rim = jnp.pad(rim, ((0, 0), (8 - (taps - 1), 0), (0, 0)))
    start = init_state.reshape(prompts, groups * gwidth, ns)
    sc = jnp.concatenate([jnp.stack([c, u]).astype(jnp.int32), lengths])

    x_in = [inner_x] + ([x_other] if per == 2 else [])
    bc_in = [bc_flat] + ([bc_other] if per == 2 else [])
    T = unit_tokens
    spec = pl.BlockSpec

    def front(s, dts):
        in_specs = [spec((1, tokens, bw), lambda k, sc: (s, 0, sc[0] * per_prompt + k))]
        in_specs += [spec((1, tokens, bw), lambda k, sc: (s, 0, k))] * (per - 1)
        in_specs += [spec((1, tokens, pair), lambda k, sc: (s, 0, sc[0]))]
        in_specs += [spec((1, tokens, pair), lambda k, sc: (s, 0, 0))] * (per - 1)
        in_specs += [spec((1, heads, tokens), lambda k, sc: (s, sc[0], 0))]
        in_specs += [spec((1, heads, tokens), lambda k, sc: (s, 0, 0))] * (per - 1)
        in_specs += [
            spec((1, 8, bw), lambda k, sc: (s, 0, k)),
            spec((1, 8, pair), lambda k, sc: (s, 0, 0)),
            spec((heads, lanes), lambda k, sc: (0, 0)),
            spec((taps, bw), lambda k, sc: (0, sc[0] * per_prompt + k)),
            spec((taps, pair), lambda k, sc: (0, sc[0])),
            spec((1, bw), lambda k, sc: (0, sc[0] * per_prompt + k)),
            spec((1, pair), lambda k, sc: (0, sc[0])),
            spec((1, bw, ns), lambda k, sc: (s, sc[0] * per_prompt + k, 0)),
        ]
        chunk = lambda k, sc: (k, 0, 0)
        whole = lambda k, sc: (0, 0, 0)
        return pl.pallas_call(
            functools.partial(front_kernel, per, hd, s),
            grid_spec=pltpu.PrefetchScalarGridSpec(
                num_scalar_prefetch=1,
                grid=(per_prompt,),
                in_specs=in_specs,
                out_specs=[
                    spec((1, T, bw), lambda k, sc: (0, 0, k)),
                    spec((1, T, pair), whole),
                    spec((1, heads, T), whole),
                    spec((1, heads, T), whole),
                    spec((1, T, lanes), whole),
                    spec((1, ns, bw), chunk),
                    spec((1, 8, bw), chunk),
                    spec((1, ns, bw), chunk),
                ],
                scratch_shapes=[
                    pltpu.VMEM((T + 8, bw), f32),
                    pltpu.VMEM((T + 8, pair), f32),
                    pltpu.VMEM((ns, T), f32),
                ],
            ),
            out_shape=[
                jax.ShapeDtypeStruct((1, T, gwidth), f32),
                jax.ShapeDtypeStruct((1, T, pair), f32),
                jax.ShapeDtypeStruct((1, heads, T), f32),
                jax.ShapeDtypeStruct((1, heads, T), f32),
                jax.ShapeDtypeStruct((1, T, lanes), f32),
                jax.ShapeDtypeStruct((per_prompt, ns, bw), f32),
                jax.ShapeDtypeStruct((per_prompt, 8, bw), f32),
                jax.ShapeDtypeStruct((per_prompt, ns, bw), bf16),
            ],
            compiler_params=params(),
            cost_estimate=cost(9),
            name="front",
        )(sc, *x_in, *bc_in, *dts, rim[..., :gwidth], rim[..., gwidth:], col, conv_x, cbc, bx, bbc, start)

    def local_part(s, k, act):
        _, bc, run, step, pack = fronts[s][:5]
        return pl.pallas_call(
            functools.partial(local_kernel, hd, k),
            grid=(1,),
            in_specs=[
                spec((1, T, bw), lambda i: (0, 0, k)),
                spec((1, T, pair), lambda i: (0, 0, 0)),
                spec((1, heads, T), lambda i: (0, 0, 0)),
                spec((1, heads, T), lambda i: (0, 0, 0)),
                spec((1, T, lanes), lambda i: (0, 0, 0)),
                spec((1, bw), lambda i: (0, k)),
            ],
            out_specs=spec((1, T, bw), lambda i: (0, 0, 0)),
            out_shape=jax.ShapeDtypeStruct((1, T, bw), f32),
            scratch_shapes=[pltpu.VMEM((T, T), f32)],
            compiler_params=params(),
            cost_estimate=cost(5),
            name="local",
        )(act, bc, run, step, pack, skip)

    fronts = [list(front(0, dt_in))]
    after_front = fronts[0][5]
    _, lengths_late = tied(after_front, lengths)
    _, dec_x = tied(after_front, dec_x)
    _, dec_bc = tied(after_front, dec_bc)
    _, dec_z = tied(after_front, dec_z)
    _, dec_dt = tied(after_front, dec_dt)
    _, row_prompt = tied(after_front, row_prompt)
    want = jnp.arange(8, dtype=jnp.int32)
    target = lengths_late[:, None] - (taps - 1) + want
    target = jnp.where(want < taps - 1, target, -1)
    places = device * tokens + jnp.arange(tokens, dtype=jnp.int32)
    hit = places[None, None, :] == target[:, :, None]
    same = jnp.arange(prompts)[:, None] == jnp.arange(prompts)[None, :]
    picker = (hit[:, :, None, :] & same[:, None, :, None]).astype(bf16)
    picker = picker.reshape(prompts * 8, prompts * tokens)
    tail_x = jnp.dot(picker, inner_x.reshape(-1, width), preferred_element_type=f32).astype(bf16)
    tail_bc = jnp.dot(
        picker, bc_flat.reshape(-1, groups * pair), preferred_element_type=f32
    ).astype(bf16)

    def tail_of(g):
        return jnp.concatenate(
            [
                lax.dynamic_slice_in_dim(tail_x, g * gwidth, gwidth, 1),
                lax.dynamic_slice_in_dim(tail_bc, g * pair, pair, 1),
            ],
            axis=1,
        )

    tails = tail_of(c)
    dec_bc = dec_bc.reshape(steps, batch, groups * pair)
    small = jnp.concatenate(
        [
            jnp.pad(jnp.transpose(dec_dt, (0, 2, 1)), ((0, 0), (0, 0), (0, lanes - groups * heads))),
            jnp.broadcast_to(row_prompt.astype(f32)[None, :, None], (1, batch, lanes)),
        ],
        axis=0,
    )
    small = [small]
    dec_other = []
    if per == 2:
        tails = tails + swap(tail_of(1 - c))
        small.append(swap(small[0]))
        dec_other = [
            swap(
                jnp.concatenate(
                    [
                        lax.dynamic_slice_in_dim(dec_x, (1 - c) * gwidth, gwidth, 2),
                        lax.dynamic_slice_in_dim(dec_bc, (1 - c) * pair, pair, 2),
                        lax.dynamic_slice_in_dim(dec_z, (1 - c) * gwidth, gwidth, 2),
                    ],
                    axis=2,
                )
            )
        ]
    tails = [tails] + [shift(tails, k) for k in range(1, m)]
    par = jnp.pad(
        jnp.stack([jnp.exp(a_log), dt_bias, d_skip]), ((0, 5), (0, lanes - groups * heads))
    )
    asked_rows = steps * rows_u

    def full_spec(arr):
        return spec(arr.shape, lambda *_: (0,) * arr.ndim)

    def window(first):
        _, late = tied(first, par)
        last = spec((1, 8, lanes), lambda i, sc: (0, T // 8 - 1, 0))
        return pl.pallas_call(
            functools.partial(window_kernel, per, hd, heads),
            grid_spec=pltpu.PrefetchScalarGridSpec(
                num_scalar_prefetch=1,
                grid=(1,),
                in_specs=[
                    spec((steps, batch, gwidth), lambda i, sc: (0, 0, sc[0])),
                    spec((steps, batch, pair), lambda i, sc: (0, 0, sc[0])),
                ]
                + [full_spec(a) for a in dec_other + small + tails]
                + [last, last, full_spec(par)]
                + [
                    spec((taps, gwidth), lambda i, sc: (0, sc[0])),
                    spec((taps, pair), lambda i, sc: (0, sc[0])),
                    spec((1, gwidth), lambda i, sc: (0, sc[0])),
                    spec((1, pair), lambda i, sc: (0, sc[0])),
                ],
                out_specs=[
                    spec((asked_rows, gwidth), lambda i, sc: (0, 0)),
                    spec((asked_rows, lanes), lambda i, sc: (0, 0)),
                    spec((asked_rows + 8, ns + lanes), lambda i, sc: (0, 0)),
                ],
            ),
            out_shape=[
                jax.ShapeDtypeStruct((asked_rows, gwidth), f32),
                jax.ShapeDtypeStruct((asked_rows, lanes), f32),
                jax.ShapeDtypeStruct((asked_rows + 8, ns + lanes), f32),
            ],
            compiler_params=params(),
            cost_estimate=cost(2),
            name="window",
        )(sc, dec_x, dec_bc, *dec_other, *small, *tails, fronts[0][4], fronts[1][4], late,
          conv_x, cbc, bx, bbc)

    def read(blocks, first):
        _, blocks[0] = tied(first, blocks[0])
        return pl.pallas_call(
            functools.partial(read_kernel, hd, heads, m),
            grid_spec=pltpu.PrefetchScalarGridSpec(
                num_scalar_prefetch=1,
                grid=(per_prompt,),
                in_specs=[full_spec(b) for b in blocks]
                + [spec((1, ns, bw), lambda k, sc: (k, 0, 0))] * prompts,
                out_specs=[spec((asked_rows, bw), lambda k, sc: (0, k))] * m,
            ),
            out_shape=[jax.ShapeDtypeStruct((asked_rows, gwidth), bf16)] * m,
            compiler_params=params(),
            cost_estimate=cost(4),
            name="read",
        )(sc, *blocks, *[f[5] for f in fronts])

    def finish(sums, local, grow):
        return pl.pallas_call(
            functools.partial(finish_kernel, per, hd, heads, m),
            grid_spec=pltpu.PrefetchScalarGridSpec(
                num_scalar_prefetch=1,
                grid=(1,),
                in_specs=[full_spec(a) for a in (*sums, local, grow)]
                + [spec((steps, batch, gwidth), lambda i, sc: (0, 0, sc[0]))]
                + [full_spec(a) for a in dec_other + [gain]],
                out_specs=spec((asked_rows, gwidth), lambda i, sc: (0, 0)),
            ),
            out_shape=jax.ShapeDtypeStruct((asked_rows, gwidth), bf16),
            compiler_params=params(),
            cost_estimate=cost(3),
            name="finish",
        )(sc, *sums, local, grow, dec_z, *dec_other, gain)

    def project(blocks):
        others = [swap(b) for b in blocks] if per == 2 else []
        cb = min(256, cols)
        return pl.pallas_call(
            functools.partial(project_kernel, per, m),
            grid_spec=pltpu.PrefetchScalarGridSpec(
                num_scalar_prefetch=1,
                grid=(cols // cb,),
                in_specs=[full_spec(b) for b in blocks + others]
                + [spec((width, cb), lambda i, sc: (0, i))],
                out_specs=spec((tp, steps, m * rows_u // tp, cb), lambda i, sc: (0, 0, 0, i)),
            ),
            out_shape=jax.ShapeDtypeStruct((tp, steps, m * rows_u // tp, cols), f32),
            compiler_params=params(),
            cost_estimate=cost(6),
            name="project",
        )(sc, *blocks, *others, w_out)

    arrived, y_local, outs = [], [], []

    def back(s, first):
        entry = []
        for k in range(s * per_prompt, (s + 1) * per_prompt):
            e = fronts[s][7][k % per_prompt]
            for v in range(1, m):
                e = jnp.where(u == v, arrived[k + v - 1], e)
            entry.append(e)
        _, pack = tied(first, fronts[s][4])
        z_in = [gate_z] + ([z_other] if per == 2 else [])
        z_specs = [spec((1, tokens, gwidth), lambda j, sc: (s, 0, sc[0]))]
        z_specs += [spec((1, tokens, gwidth), lambda j, sc: (s, 0, 0))] * (per - 1)
        return pl.pallas_call(
            functools.partial(back_kernel, per, hd, heads),
            grid_spec=pltpu.PrefetchScalarGridSpec(
                num_scalar_prefetch=1,
                grid=(per,),
                in_specs=z_specs
                + [spec((1, ns, bw), lambda j, sc: (0, 0, 0))] * per_prompt
                + [
                    spec((1, tokens, pair), lambda j, sc: (0, j, 0)),
                    spec((1, tokens, lanes), lambda j, sc: (0, j, 0)),
                    spec((1, gwidth), lambda j, sc: (0, 0)),
                ]
                + [spec((1, tokens, bw), lambda j, sc: (0, j, 0))] * per_prompt,
                out_specs=spec(
                    (1, tokens, gwidth), lambda j, sc: (jnp.where(j == sc[0], 0, 1), 0, 0)
                ),
                scratch_shapes=[pltpu.VMEM((tokens, gwidth), f32)],
            ),
            out_shape=jax.ShapeDtypeStruct((per, tokens, gwidth), bf16),
            compiler_params=params(60 * 1024 * 1024),
            cost_estimate=cost(5),
            name="back",
        )(
            sc,
            *z_in,
            *[e[None] for e in entry],
            fronts[s][1],
            pack,
            gain,
            *y_local[s * per_prompt : (s + 1) * per_prompt],
        )

    carry = jnp.zeros((ns, bw), bf16)
    along = [(i, i + per) for i in range(n - per)]

    def locals_after(first, count, moved):
        for _ in range(count):
            s, k = divmod(len(y_local), per_prompt)
            if s == prompts:
                break
            _, act = tied(first, fronts[s][0])
            first = local_part(s, k, act)
            y_local.append(first)
            moved, _ = tied(moved, first)
        return moved

    for t in range(parts + m - 2):
        at_k = jnp.clip(t - u, 0, parts - 1)
        leave = None
        for s in range(prompts - 1, -1, -1):
            if t < s * per_prompt:
                continue
            at_s = jnp.clip(at_k - s * per_prompt, 0, per_prompt - 1)
            own_t = lax.dynamic_index_in_dim(fronts[s][5], at_s, 0, keepdims=False)
            decay_t = lax.dynamic_index_in_dim(fronts[s][6], at_s, 0, keepdims=False)[:1]
            new = (decay_t * carry.astype(f32) + own_t).astype(bf16)
            leave = new if leave is None else jnp.where(at_k < (s + 1) * per_prompt, new, leave)
        moved = lax.ppermute(leave, "ctx", along)
        if t == 0:
            for s in range(1, prompts):
                _, sc = tied(leave, sc)
                fronts.append(list(front(s, dt_in)))
            moved, _ = tied(moved, fronts[-1][5])
        if t == 1:
            moved = locals_after(leave, 1, moved)
            local, grow, payload = window(y_local[-1])
            blocks = [payload] + [shift(payload, k) for k in range(1, m)]
            moved = locals_after(payload, 1, moved)
        if t == 2:
            sends = list(read(blocks, leave))
            sums = sends[:1] + [shift(sends[k], -k) for k in range(1, m)]
            _, gate_late = tied(sends[-1], gate_z)
            z_other = other_group(gate_late, gwidth)
            moved = locals_after(sends[-1], 1, moved)
        if t == 3:
            moved = locals_after(leave, 1, moved)
            _, sums[0] = tied(y_local[-1], sums[0])
            hidden = finish(sums, local, grow)
            moved, _ = tied(moved, hidden)
            if per == 2:
                moved, _ = tied(moved, z_other)
        if t == 4:
            around = [hidden] + [shift(hidden, k) for k in range(1, m)]
            for got in around:
                moved, _ = tied(moved, got)
        if t == 5:
            _, around[0] = tied(leave, around[0])
            product = project(around)
            terms = lax.all_to_all(product, "tp", 0, 0)
        if t == per_prompt + m - 2:
            outs.append(back(0, leave))
            moved, _ = tied(moved, outs[0])
        if t == parts + m - 3:
            moved, _ = tied(moved, product)
        carry = moved
        arrived.append(carry)
    while len(y_local) < parts:
        done = len(y_local)
        y_local.append(local_part(done // per_prompt, done % per_prompt, fronts[done // per_prompt][0]))

    layer_out = jnp.sum(terms, axis=0).astype(bf16)
    for s in range(1, prompts):
        outs.append(back(s, carry))
    full_outs = []
    for out in outs:
        if per == 1:
            full_outs.append(out[0])
            continue
        given = swap(out[1])
        _, kept = tied(layer_out, out[0])
        full_outs.append(in_order(kept, given, 1))
    return (jnp.stack(full_outs), layer_out)


def solution(mesh):
    in_specs = (
        P(None, "ctx", "tp"),
        P(None, "ctx", "tp"),
        P(None, "ctx", "tp", None),
        P(None, "tp", "ctx"),
        P("tp"),
        P("tp"),
        P("tp"),
        P(None, "tp"),
        P(None, "tp", None),
        P("tp"),
        P("tp", None),
        P("tp"),
        P(None, "tp", None, None),
        P(None, None, "tp"),
        P(None, None, "tp", None),
        P(),
        P(None, "ctx", "tp"),
        P(None, "ctx", "tp"),
        P(None, "ctx", "tp", None),
        P(None, "tp", "ctx"),
        P("ctx"),
        P("tp", "ctx"),
    )
    out_specs = (P(None, "ctx", "tp"), P(None, "tp", "ctx"))
    return jax.shard_map(shards, mesh=mesh, in_specs=in_specs, out_specs=out_specs, check_vma=False)
```

```python
import functools

import jax
import jax.numpy as jnp
from jax import lax
from jax.experimental import pallas as pl
from jax.experimental.pallas import tpu as pltpu
from jax.sharding import PartitionSpec as P

epsilon = 1e-05
highest = lax.Precision.HIGHEST
f32, bf16 = jnp.float32, jnp.bfloat16
lanes = 128
vmem = 40 * 1024 * 1024


def silu(v):
    return v * (1.0 / (1.0 + jnp.exp(-v)))


def softplus(v):
    return jnp.maximum(v, 0.0) + jnp.log1p(jnp.exp(-jnp.abs(v)))


def exact(a, b):
    return jnp.dot(a, b, precision=highest, preferred_element_type=f32)


def exact_t(a, b):
    return lax.dot_general(
        a, b, (((1,), (1,)), ((), ())), precision=highest, preferred_element_type=f32
    )


def one_pass(a, b):
    return jnp.dot(a, b, preferred_element_type=f32)


def halves(a):
    high = a.astype(bf16)
    return high, (a - high.astype(f32)).astype(bf16)


def three_pass(a, b):
    a_hi, a_lo = halves(a)
    b_hi, b_lo = halves(b)
    return one_pass(a_hi, b_hi) + (one_pass(a_lo, b_hi) + one_pass(a_hi, b_lo))


def spread_out(a, picks):
    high, low = halves(a)
    return one_pass(high, picks) + one_pass(low, picks)


def to_channels(columns, hd, first):
    row = lax.broadcasted_iota(jnp.int32, (lanes, columns), 0)
    col = lax.broadcasted_iota(jnp.int32, (lanes, columns), 1)
    return (row == col // hd + first).astype(bf16)


def joined(refs, c, axis=0):
    if len(refs) == 1:
        return refs[0][0]
    a, b = refs[0][0], refs[1][0]
    return jnp.concatenate([jnp.where(c == 0, a, b), jnp.where(c == 0, b, a)], axis=axis)


def convolved(scratch, rim, body, taps_ref, bias_ref):
    rows = body.shape[0]
    taps = taps_ref.shape[0]
    scratch[0:8] = rim
    scratch[8 : 8 + rows] = body
    total = bias_ref[...]
    for k in range(taps):
        start = 8 - (taps - 1) + k
        total = total + taps_ref[k : k + 1] * scratch[start : start + rows]
    return silu(total)


def front_kernel(per, hd, prompt, sc, *refs):
    x_refs, refs = refs[:per], refs[per:]
    bc_refs, refs = refs[:per], refs[per:]
    dt_refs, refs = refs[:per], refs[per:]
    (rim_x, rim_bc, col, cx, cbc, bx, bbc, start) = refs[:8]
    (act_o, bc_o, run_o, step_o, pack_o, own_o, dec_o, start_o) = refs[8:16]
    xs, bs, bt = refs[16:]
    half = pl.program_id(0)
    c, u = sc[0], sc[1]
    _, heads, rows = run_o.shape
    n = bt.shape[0]
    bw = act_o.shape[2]

    @pl.when(half == 0)
    def _():
        at = u * rows + lax.broadcasted_iota(jnp.int32, (heads, rows), 1)
        live = jnp.where(at < sc[2 + prompt], 1.0, 0.0)
        step = softplus(joined(dt_refs, c, 1) + col[:, 1:2]) * live
        i = lax.broadcasted_iota(jnp.int32, (rows, rows), 0)
        j = lax.broadcasted_iota(jnp.int32, (rows, rows), 1)
        run = exact(-col[:, 0:1] * step, (i <= j).astype(f32))
        to_end = jnp.exp(run[:, rows - 1 :] - run) * step
        run_o[0] = run
        step_o[0] = step
        pack_o[0] = jnp.transpose(jnp.concatenate([to_end, jnp.exp(run), run, step], axis=0))
        bc = convolved(bs, rim_bc[0], joined(bc_refs, c).astype(f32), cbc, bbc)
        bc_o[0] = bc
        bt[...] = jnp.transpose(bc[:, :n])

    act = convolved(xs, rim_x[0], joined(x_refs, c).astype(f32), cx, bx)
    act_o[0] = act
    first = half * (bw // hd)
    weighted = act * spread_out(pack_o[0], to_channels(bw, hd, first))
    own = three_pass(bt[...], weighted)
    decay = spread_out(pack_o[0, rows - 8 :, :], to_channels(bw, hd, first + heads))[7:8]
    dec_o[0] = jnp.broadcast_to(decay, (8, bw))

    @pl.when(u == 0)
    def _():
        begin = jnp.transpose(start[0])
        own_o[0] = own + decay * begin
        start_o[0] = begin.astype(bf16)

    @pl.when(u != 0)
    def _():
        own_o[0] = own
        start_o[0] = jnp.zeros(start_o.shape[1:], bf16)


def local_kernel(hd, at_part, act, bc, run, step, pack, skip, y_o, scores):
    half = pl.program_id(0) + at_part
    heads, rows = run.shape[1:]
    bw = act.shape[2]
    n = bc.shape[2] // 2

    scores[...] = exact_t(bc[0, :, n:], bc[0, :, :n])

    i = lax.broadcasted_iota(jnp.int32, (rows, rows), 0)
    j = lax.broadcasted_iota(jnp.int32, (rows, rows), 1)
    lower = i >= j
    lane = lax.broadcasted_iota(jnp.int32, (rows, lanes), 1)
    each = lanes // hd
    first = half * (bw // hd)

    def block(q, carry):
        at = pl.ds(pl.multiple_of(q * lanes, lanes), lanes)
        x = act[0, :, at]
        x_hi, x_lo = halves(x)
        y = skip[:, at] * x
        for e in range(each):
            h = first + q * each + e
            column = jnp.sum(jnp.where(lane == h + 2 * heads, pack[0], 0.0), axis=1, keepdims=True)
            gap = column - run[0, pl.ds(h, 1), :]
            mixing = jnp.exp(jnp.where(lower, gap, -1e30)) * (scores[...] * step[0, pl.ds(h, 1), :])
            m_hi, m_lo = halves(mixing)
            got = one_pass(m_hi, x_hi) + (one_pass(m_lo, x_hi) + one_pass(m_hi, x_lo))
            y = y + jnp.where(lane // hd == e, got, 0.0)
        y_o[0, :, at] = y
        return carry

    lax.fori_loop(0, bw // lanes, block, 0)


def back_kernel(per, hd, heads, sc, *refs):
    g_refs, refs = refs[:per], refs[per:]
    outs, mixed = refs[-1 - per : -1], refs[-1]
    rest = refs[: -1 - per]
    parts = (len(rest) - 3) // 2
    entry, (bc, pack, gain), local = rest[:parts], rest[parts : parts + 3], rest[parts + 3 :]
    token_block = pl.program_id(0)
    c = sc[0]
    _, n, bw = entry[0].shape
    gate = g_refs[0][0]
    if per == 2:
        gate = jnp.where(token_block == c, gate, g_refs[1][0])
    c_hi, c_lo = halves(bc[0, :, n:])
    total = None
    for k in range(parts):
        at = slice(k * bw, (k + 1) * bw)
        seen = one_pass(c_hi, entry[k][0]) + one_pass(c_lo, entry[k][0])
        grow = spread_out(pack[0], to_channels(bw, hd, heads + k * (bw // hd)))
        y = local[k][0] + grow * seen
        v = y * silu(gate[:, at].astype(f32))
        mixed[:, at] = v
        square = jnp.sum(v * v, axis=1, keepdims=True)
        total = square if total is None else total + square
    scale = lax.rsqrt(total / (parts * bw) + epsilon)
    out = (mixed[...] * scale * gain[...]).astype(bf16)
    if per == 1:
        outs[0][...] = out
        return

    @pl.when(token_block == c)
    def _():
        outs[0][...] = out

    @pl.when(token_block != c)
    def _():
        outs[1][...] = out


def rows_of(refs, i, at, c):
    a = refs[0][i][:, at[0]].astype(f32)
    if len(refs) == 1:
        return a
    b = refs[1][i][:, at[1]].astype(f32)
    return jnp.concatenate([jnp.where(c == 0, a, b), jnp.where(c == 0, b, a)], axis=0)


def window_kernel(per, hd, heads, sc, *refs):
    x_ref, bc_ref, refs = refs[0], refs[1], refs[2:]
    other, refs = refs[: per - 1], refs[per - 1 :]
    small, refs = refs[:per], refs[per:]
    *tails, last0, last1, par, cx, cbc, bx, bbc, local_o, grow_o, pay_o = refs
    c = sc[0]
    taps = cx.shape[0]
    steps, batch, gwidth = x_ref.shape
    pair = bc_ref.shape[2]
    ns = pair // 2
    rows = per * batch
    whole = slice(None)
    tail = sum(t[...].astype(f32) for t in tails)
    prompt = rows_of(small, steps, (whole, whole), c)
    body_x = [rows_of([x_ref, *other], i, (whole, slice(0, gwidth)), c) for i in range(steps)]
    body_bc = [
        rows_of([bc_ref, *other], i, (whole, slice(gwidth, gwidth + pair)), c) for i in range(steps)
    ]

    def window(lo, hi, body):
        out = []
        for j in range(taps - 1):
            first, second = tail[j : j + 1, lo:hi], tail[8 + j : 9 + j, lo:hi]
            out.append(jnp.where(prompt[:, :1] == 0.0, first, second))
        return out + body

    def conv(full, taps_ref, bias):
        acts = []
        for i in range(steps):
            total = bias
            for k in range(taps):
                total = total + taps_ref[k : k + 1] * full[i + k]
            acts.append(silu(total))
        return acts

    xd = conv(window(0, gwidth, body_x), cx, bx[...])
    mix = conv(window(gwidth, gwidth + pair, body_bc), cbc, bbc[...])
    rate, dtb, skip = par[0:1], par[1:2], par[2:3]
    step = [softplus(rows_of(small, i, (whole, whole), c) + dtb) for i in range(steps)]
    upto = []
    for i in range(steps):
        upto.append((upto[-1] if upto else 0.0) - rate * step[i])
    coef = [jnp.broadcast_to(skip, (8, lanes))]
    for i in range(steps):
        read = mix[i][:, ns:]
        pay_o[i * rows : (i + 1) * rows, :ns] = read
        pay_o[i * rows : (i + 1) * rows, ns:] = prompt
        grow_o[i * rows : (i + 1) * rows] = jnp.exp(upto[i])
        for j in range(i + 1):
            both = jnp.sum(read * mix[j][:, :ns], axis=1, keepdims=True)
            coef.append(both * (jnp.exp(upto[i] - upto[j]) * step[j]))
    wide = spread_out(jnp.concatenate(coef, axis=0), to_channels(gwidth, hd, c * heads))
    at = 8
    for i in range(steps):
        y = wide[0:1] * xd[i]
        for j in range(i + 1):
            y = y + wide[at : at + rows] * xd[j]
            at += rows
        local_o[i * rows : (i + 1) * rows] = y
    pay_o[steps * rows :, :ns] = jnp.zeros((8, ns), f32)
    pay_o[steps * rows :, ns:] = jnp.concatenate(
        [last0[0, 7:8], last1[0, 7:8], jnp.zeros((6, lanes), f32)], axis=0
    )


def read_kernel(hd, heads, order, sc, *refs):
    m = len(order)
    blocks, own, outs = refs[:m], refs[m:-2], refs[-2:]
    half = pl.program_id(0)
    _, ns, bw = own[0].shape
    u = sc[1]
    rows = blocks[0].shape[0] - 8
    after = jnp.zeros((8, lanes), f32)
    for k, block in zip(order[1:], blocks[1:]):
        after = after + jnp.where((u ^ k) > u, block[rows:, ns:], 0.0)
    spread = spread_out(jnp.exp(after), to_channels(bw, hd, 2 * heads + half * (bw // hd)))
    asked = jnp.concatenate([b[:rows, :ns] for b in blocks], axis=0)
    prompt = jnp.concatenate([b[:rows, ns : ns + 1] for b in blocks], axis=0)
    total = None
    for s in range(len(own)):
        c_hi, c_lo = halves(jnp.where(prompt == s, asked, 0.0))
        s_hi, s_lo = halves(own[s][0] * spread[s : s + 1])
        got = one_pass(c_hi, s_hi) + (one_pass(c_lo, s_hi) + one_pass(c_hi, s_lo))
        total = got if total is None else total + got
    outs[0][...] = total[: m // 2 * rows].astype(bf16)
    outs[1][...] = total[m // 2 * rows :].astype(bf16)


def finish_kernel(per, hd, heads, sc, *refs):
    m = 2
    sums, local, grow, z_ref, refs = refs[:m], refs[m], refs[m + 1], refs[m + 2], refs[m + 3 :]
    *other, gain, out_o = refs
    c = sc[0]
    steps = z_ref.shape[0]
    gwidth = out_o.shape[1]
    total = sums[0][...].astype(f32)
    for r in sums[1:]:
        total = total + r[...].astype(f32)
    y = spread_out(grow[...], to_channels(gwidth, hd, c * heads)) * total + local[...]
    at = (slice(None), slice(other[0].shape[2] - gwidth, None) if other else None)
    gate = jnp.concatenate([rows_of([z_ref, *other], i, at, c) for i in range(steps)], axis=0)
    v = y * silu(gate)
    scale = lax.rsqrt(jnp.mean(v * v, axis=1, keepdims=True) + epsilon)
    out_o[...] = (v * scale * gain[...]).astype(bf16)


def project_kernel(per, order, sc, *refs):
    m = len(order)
    mine, other, w, out_o = refs[:m], refs[m:-2], refs[-2], refs[-1]
    c, u = sc[0], sc[1]
    tp, steps, rows_tp, cols = out_o.shape
    a = jnp.concatenate([r[...] for r in mine], axis=0)
    gwidth = a.shape[1]
    if per == 2:
        b = jnp.concatenate([r[...] for r in other], axis=0)
        total = one_pass(jnp.where(c == 0, a, b), w[:gwidth])
        total = total + one_pass(jnp.where(c == 0, b, a), w[gwidth:])
    else:
        total = one_pass(a, w[...])
    rows = a.shape[0] // (m * steps)
    each = m // tp
    for place, k in enumerate(order):
        v = u ^ k
        at = pl.ds(pl.multiple_of(lax.rem(v, each) * rows, rows), rows)
        for i in range(steps):
            first = (place * steps + i) * rows
            out_o[v // each, i, at, :] = total[first : first + rows]


def params(limit=vmem):
    return pltpu.CompilerParams(vmem_limit_bytes=limit)


def cost(us):
    return pl.CostEstimate(flops=int(us * 1.1e9), bytes_accessed=int(us * 3e6), transcendentals=0)


def tied(first, then):
    return lax.optimization_barrier((first, then))


def shards(
    inner_x,
    gate_z,
    proj_bc,
    dt_raw,
    a_log,
    dt_bias,
    d_skip,
    conv_x,
    conv_bc,
    bias_x,
    bias_bc,
    norm_gain,
    init_state,
    init_conv_x,
    init_conv_bc,
    lengths,
    dec_x,
    dec_z,
    dec_bc,
    dec_dt,
    row_prompt,
    w_out,
):
    prompts, tokens, width = inner_x.shape
    groups, pair = proj_bc.shape[2:]
    ns = pair // 2
    heads = dt_raw.shape[1] // groups
    gwidth = width // groups
    hd = gwidth // heads
    taps = conv_x.shape[0]
    steps, batch = dec_x.shape[:2]
    cols = w_out.shape[1]
    n = lax.axis_size("ctx")
    tp = lax.axis_size("tp")
    assert groups in (1, 2) and n % groups == 0 and 4 * heads == lanes
    per = groups
    m = n // per
    device = lax.axis_index("ctx")
    u, c = device // per, device % per
    unit_tokens = per * tokens
    rows_u = per * batch
    per_prompt = 2
    bw = gwidth // per_prompt
    parts = prompts * per_prompt

    def mine(arr, axis):
        return lax.dynamic_index_in_dim(arr, c, axis, keepdims=False)

    def swap(arr):
        return lax.ppermute(arr, "ctx", [(i, i ^ 1) for i in range(n)])

    def in_order(own, other, axis):
        first = jnp.where(c == 0, own, other)
        second = jnp.where(c == 0, other, own)
        return jnp.concatenate([first, second], axis=axis)

    def other_group(arr, size):
        if per == 1:
            return None
        at = [0] * (arr.ndim - 1) + [(1 - c) * size]
        return swap(lax.dynamic_slice(arr, at, arr.shape[:-1] + (size,)))

    def pair_up(arr, gaxis, taxis):
        if per == 1:
            return jnp.squeeze(arr, gaxis)
        other = swap(lax.dynamic_index_in_dim(arr, 1 - c, gaxis, keepdims=False))
        return in_order(mine(arr, gaxis), other, taxis)

    def trade(arr, k):
        return lax.ppermute(arr, "ctx", [(i, (i // per ^ k) * per + i % per) for i in range(n)])

    assert m & (m - 1) == 0
    bits = [1 << b for b in range(m.bit_length() - 1)]
    order = [0]
    for b in reversed(bits):
        order = order + [k | b for k in order]
    order = sorted(order, key=lambda k: [k >> b & 1 for b in range(len(bits))])

    bc_flat = proj_bc.reshape(prompts, tokens, groups * pair)
    x_other = bc_other = None
    if per == 2:
        x_send = lax.dynamic_slice_in_dim(inner_x, (1 - c) * gwidth, gwidth, 2)
        x_other = swap(x_send)
        bc_other = other_group(bc_flat, pair)
    last_x = inner_x[:, tokens - taps + 1 :]
    last_bc = bc_flat[:, tokens - taps + 1 :]
    wide = gwidth + pair
    rim = jnp.zeros((prompts, taps - 1, wide), bf16)
    for g in range(per):
        pairs = [(v * per + per - 1, (v + 1) * per + g) for v in range(m - 1)]
        send = jnp.concatenate(
            [last_x[..., g * gwidth : (g + 1) * gwidth], last_bc[..., g * pair : (g + 1) * pair]],
            axis=-1,
        )
        got = lax.ppermute(send, "ctx", pairs)
        rim = jnp.where(c == g, got, rim)
    lengths_late = tied(x_send, lengths)[1] if per == 2 else lengths
    want = jnp.arange(8, dtype=jnp.int32)
    target = lengths_late[:, None] - (taps - 1) + want
    target = jnp.where(want < taps - 1, target, -1)
    places = device * tokens + jnp.arange(tokens, dtype=jnp.int32)
    hit = places[None, None, :] == target[:, :, None]
    same = jnp.arange(prompts)[:, None] == jnp.arange(prompts)[None, :]
    picker = (hit[:, :, None, :] & same[:, None, :, None]).astype(bf16)
    picker = picker.reshape(prompts * 8, prompts * tokens)
    tail_x = jnp.dot(picker, inner_x.reshape(-1, width), preferred_element_type=f32).astype(bf16)
    tail_bc = jnp.dot(
        picker, bc_flat.reshape(-1, groups * pair), preferred_element_type=f32
    ).astype(bf16)

    def tail_of(g):
        return jnp.concatenate(
            [
                lax.dynamic_slice_in_dim(tail_x, g * gwidth, gwidth, 1),
                lax.dynamic_slice_in_dim(tail_bc, g * pair, pair, 1),
            ],
            axis=1,
        )

    tails = tail_of(c)
    if per == 2:
        tails = tails + swap(tail_of(1 - c))
    dt_in = [dt_raw]
    if per == 2:
        given = lax.dynamic_slice_in_dim(dt_raw, (1 - c) * heads, heads, 1)
        dt_in.append(swap(given))

    rate = jnp.exp(mine(a_log.reshape(groups, heads), 0))
    dtb = mine(dt_bias.reshape(groups, heads), 0)
    skip = jnp.repeat(mine(d_skip.reshape(groups, heads), 0), hd)[None]
    gain = mine(norm_gain.reshape(groups, 1, gwidth), 0)
    col = jnp.pad(jnp.stack([rate, dtb], axis=1), ((0, 0), (0, lanes - 2)))
    cbc = conv_bc.reshape(taps, groups * pair)
    bbc = bias_bc.reshape(1, groups * pair)
    bx = bias_x.reshape(1, width)
    start_rim = jnp.concatenate(
        [
            mine(init_conv_x.reshape(prompts, taps - 1, groups, gwidth), 2),
            mine(init_conv_bc, 2),
        ],
        axis=-1,
    )
    rim = jnp.where(u == 0, start_rim, rim).astype(f32)
    rim = jnp.pad(rim, ((0, 0), (8 - (taps - 1), 0), (0, 0)))
    start = init_state.reshape(prompts, groups * gwidth, ns)
    sc = jnp.concatenate([jnp.stack([c, u]).astype(jnp.int32), lengths])

    x_in = [inner_x] + ([x_other] if per == 2 else [])
    bc_in = [bc_flat] + ([bc_other] if per == 2 else [])
    T = unit_tokens
    spec = pl.BlockSpec

    def front(s, dts):
        in_specs = [spec((1, tokens, bw), lambda k, sc: (s, 0, sc[0] * per_prompt + k))]
        in_specs += [spec((1, tokens, bw), lambda k, sc: (s, 0, k))] * (per - 1)
        in_specs += [spec((1, tokens, pair), lambda k, sc: (s, 0, sc[0]))]
        in_specs += [spec((1, tokens, pair), lambda k, sc: (s, 0, 0))] * (per - 1)
        in_specs += [spec((1, heads, tokens), lambda k, sc: (s, sc[0], 0))]
        in_specs += [spec((1, heads, tokens), lambda k, sc: (s, 0, 0))] * (per - 1)
        in_specs += [
            spec((1, 8, bw), lambda k, sc: (s, 0, k)),
            spec((1, 8, pair), lambda k, sc: (s, 0, 0)),
            spec((heads, lanes), lambda k, sc: (0, 0)),
            spec((taps, bw), lambda k, sc: (0, sc[0] * per_prompt + k)),
            spec((taps, pair), lambda k, sc: (0, sc[0])),
            spec((1, bw), lambda k, sc: (0, sc[0] * per_prompt + k)),
            spec((1, pair), lambda k, sc: (0, sc[0])),
            spec((1, bw, ns), lambda k, sc: (s, sc[0] * per_prompt + k, 0)),
        ]
        chunk = lambda k, sc: (k, 0, 0)
        whole = lambda k, sc: (0, 0, 0)
        return pl.pallas_call(
            functools.partial(front_kernel, per, hd, s),
            grid_spec=pltpu.PrefetchScalarGridSpec(
                num_scalar_prefetch=1,
                grid=(per_prompt,),
                in_specs=in_specs,
                out_specs=[
                    spec((1, T, bw), lambda k, sc: (0, 0, k)),
                    spec((1, T, pair), whole),
                    spec((1, heads, T), whole),
                    spec((1, heads, T), whole),
                    spec((1, T, lanes), whole),
                    spec((1, ns, bw), chunk),
                    spec((1, 8, bw), chunk),
                    spec((1, ns, bw), chunk),
                ],
                scratch_shapes=[
                    pltpu.VMEM((T + 8, bw), f32),
                    pltpu.VMEM((T + 8, pair), f32),
                    pltpu.VMEM((ns, T), f32),
                ],
            ),
            out_shape=[
                jax.ShapeDtypeStruct((1, T, gwidth), f32),
                jax.ShapeDtypeStruct((1, T, pair), f32),
                jax.ShapeDtypeStruct((1, heads, T), f32),
                jax.ShapeDtypeStruct((1, heads, T), f32),
                jax.ShapeDtypeStruct((1, T, lanes), f32),
                jax.ShapeDtypeStruct((per_prompt, ns, bw), f32),
                jax.ShapeDtypeStruct((per_prompt, 8, bw), f32),
                jax.ShapeDtypeStruct((per_prompt, ns, bw), bf16),
            ],
            compiler_params=params(),
            cost_estimate=cost(9),
            name="front",
        )(sc, *x_in, *bc_in, *dts, rim[..., :gwidth], rim[..., gwidth:], col, conv_x, cbc, bx, bbc, start)

    def local_part(s, k, act):
        _, bc, run, step, pack = fronts[s][:5]
        return pl.pallas_call(
            functools.partial(local_kernel, hd, k),
            grid=(1,),
            in_specs=[
                spec((1, T, bw), lambda i: (0, 0, k)),
                spec((1, T, pair), lambda i: (0, 0, 0)),
                spec((1, heads, T), lambda i: (0, 0, 0)),
                spec((1, heads, T), lambda i: (0, 0, 0)),
                spec((1, T, lanes), lambda i: (0, 0, 0)),
                spec((1, bw), lambda i: (0, k)),
            ],
            out_specs=spec((1, T, bw), lambda i: (0, 0, 0)),
            out_shape=jax.ShapeDtypeStruct((1, T, bw), f32),
            scratch_shapes=[pltpu.VMEM((T, T), f32)],
            compiler_params=params(),
            cost_estimate=cost(5),
            name="local",
        )(act, bc, run, step, pack, skip)

    fronts = [list(front(0, dt_in))]
    after_front = fronts[0][5]
    _, dec_x = tied(after_front, dec_x)
    _, dec_bc = tied(after_front, dec_bc)
    _, dec_z = tied(after_front, dec_z)
    _, dec_dt = tied(after_front, dec_dt)
    _, row_prompt = tied(after_front, row_prompt)
    dec_bc = dec_bc.reshape(steps, batch, groups * pair)
    small = jnp.concatenate(
        [
            jnp.pad(jnp.transpose(dec_dt, (0, 2, 1)), ((0, 0), (0, 0), (0, lanes - groups * heads))),
            jnp.broadcast_to(row_prompt.astype(f32)[None, :, None], (1, batch, lanes)),
        ],
        axis=0,
    )
    small = [small]
    dec_other = []
    if per == 2:
        small.append(swap(small[0]))
        dec_other = [
            swap(
                jnp.concatenate(
                    [
                        lax.dynamic_slice_in_dim(dec_x, (1 - c) * gwidth, gwidth, 2),
                        lax.dynamic_slice_in_dim(dec_bc, (1 - c) * pair, pair, 2),
                        lax.dynamic_slice_in_dim(dec_z, (1 - c) * gwidth, gwidth, 2),
                    ],
                    axis=2,
                )
            )
        ]
    _, tails = tied(after_front, tails)
    tails = [tails] + [trade(tails, k) for k in range(1, m)]
    par = jnp.pad(
        jnp.stack([jnp.exp(a_log), dt_bias, d_skip]), ((0, 5), (0, lanes - groups * heads))
    )
    asked_rows = steps * rows_u

    def full_spec(arr):
        return spec(arr.shape, lambda *_: (0,) * arr.ndim)

    def window(first):
        _, late = tied(first, par)
        last = spec((1, 8, lanes), lambda i, sc: (0, T // 8 - 1, 0))
        return pl.pallas_call(
            functools.partial(window_kernel, per, hd, heads),
            grid_spec=pltpu.PrefetchScalarGridSpec(
                num_scalar_prefetch=1,
                grid=(1,),
                in_specs=[
                    spec((steps, batch, gwidth), lambda i, sc: (0, 0, sc[0])),
                    spec((steps, batch, pair), lambda i, sc: (0, 0, sc[0])),
                ]
                + [full_spec(a) for a in dec_other + small + tails]
                + [last, last, full_spec(par)]
                + [
                    spec((taps, gwidth), lambda i, sc: (0, sc[0])),
                    spec((taps, pair), lambda i, sc: (0, sc[0])),
                    spec((1, gwidth), lambda i, sc: (0, sc[0])),
                    spec((1, pair), lambda i, sc: (0, sc[0])),
                ],
                out_specs=[
                    spec((asked_rows, gwidth), lambda i, sc: (0, 0)),
                    spec((asked_rows, lanes), lambda i, sc: (0, 0)),
                    spec((asked_rows + 8, ns + lanes), lambda i, sc: (0, 0)),
                ],
            ),
            out_shape=[
                jax.ShapeDtypeStruct((asked_rows, gwidth), f32),
                jax.ShapeDtypeStruct((asked_rows, lanes), f32),
                jax.ShapeDtypeStruct((asked_rows + 8, ns + lanes), f32),
            ],
            compiler_params=params(),
            cost_estimate=cost(2),
            name="window",
        )(sc, dec_x, dec_bc, *dec_other, *small, *tails, fronts[0][4], fronts[1][4], late,
          conv_x, cbc, bx, bbc)

    def read(blocks, first):
        _, blocks[0] = tied(first, blocks[0])
        return pl.pallas_call(
            functools.partial(read_kernel, hd, heads, order),
            grid_spec=pltpu.PrefetchScalarGridSpec(
                num_scalar_prefetch=1,
                grid=(per_prompt,),
                in_specs=[full_spec(b) for b in blocks]
                + [spec((1, ns, bw), lambda k, sc: (k, 0, 0))] * prompts,
                out_specs=[spec((m // 2 * asked_rows, bw), lambda k, sc: (0, k))] * 2,
            ),
            out_shape=[jax.ShapeDtypeStruct((m // 2 * asked_rows, gwidth), bf16)] * 2,
            compiler_params=params(),
            cost_estimate=cost(4),
            name="read",
        )(sc, *blocks, *[f[5] for f in fronts])

    def finish(sums, local, grow):
        return pl.pallas_call(
            functools.partial(finish_kernel, per, hd, heads),
            grid_spec=pltpu.PrefetchScalarGridSpec(
                num_scalar_prefetch=1,
                grid=(1,),
                in_specs=[full_spec(a) for a in (*sums, local, grow)]
                + [spec((steps, batch, gwidth), lambda i, sc: (0, 0, sc[0]))]
                + [full_spec(a) for a in dec_other + [gain]],
                out_specs=spec((asked_rows, gwidth), lambda i, sc: (0, 0)),
            ),
            out_shape=jax.ShapeDtypeStruct((asked_rows, gwidth), bf16),
            compiler_params=params(),
            cost_estimate=cost(3),
            name="finish",
        )(sc, *sums, local, grow, dec_z, *dec_other, gain)

    def project(blocks):
        others = [swap(b) for b in blocks] if per == 2 else []
        cb = min(256, cols)
        return pl.pallas_call(
            functools.partial(project_kernel, per, order),
            grid_spec=pltpu.PrefetchScalarGridSpec(
                num_scalar_prefetch=1,
                grid=(cols // cb,),
                in_specs=[full_spec(b) for b in blocks + others]
                + [spec((width, cb), lambda i, sc: (0, i))],
                out_specs=spec((tp, steps, m * rows_u // tp, cb), lambda i, sc: (0, 0, 0, i)),
            ),
            out_shape=jax.ShapeDtypeStruct((tp, steps, m * rows_u // tp, cols), f32),
            compiler_params=params(60 * 1024 * 1024),
            cost_estimate=cost(6),
            name="project",
        )(sc, *blocks, *others, w_out)

    arrived, y_local, outs = [], [], []

    def back(s, first):
        entry = []
        for k in range(s * per_prompt, (s + 1) * per_prompt):
            e = fronts[s][7][k % per_prompt]
            for v in range(1, m):
                e = jnp.where(u == v, arrived[k + v - 1], e)
            entry.append(e)
        _, pack = tied(first, fronts[s][4])
        z_in = [gate_z] + ([z_other] if per == 2 else [])
        z_specs = [spec((1, tokens, gwidth), lambda j, sc: (s, 0, sc[0]))]
        z_specs += [spec((1, tokens, gwidth), lambda j, sc: (s, 0, 0))] * (per - 1)
        return pl.pallas_call(
            functools.partial(back_kernel, per, hd, heads),
            grid_spec=pltpu.PrefetchScalarGridSpec(
                num_scalar_prefetch=1,
                grid=(per,),
                in_specs=z_specs
                + [spec((1, ns, bw), lambda j, sc: (0, 0, 0))] * per_prompt
                + [
                    spec((1, tokens, pair), lambda j, sc: (0, j, 0)),
                    spec((1, tokens, lanes), lambda j, sc: (0, j, 0)),
                    spec((1, gwidth), lambda j, sc: (0, 0)),
                ]
                + [spec((1, tokens, bw), lambda j, sc: (0, j, 0))] * per_prompt,
                out_specs=[spec((tokens, gwidth), lambda j, sc: (0, 0))] * per,
                scratch_shapes=[pltpu.VMEM((tokens, gwidth), f32)],
            ),
            out_shape=[jax.ShapeDtypeStruct((tokens, gwidth), bf16)] * per,
            compiler_params=params(60 * 1024 * 1024),
            cost_estimate=cost(5),
            name="back",
        )(
            sc,
            *z_in,
            *[e[None] for e in entry],
            fronts[s][1],
            pack,
            gain,
            *y_local[s * per_prompt : (s + 1) * per_prompt],
        )

    carry = jnp.zeros((ns, bw), bf16)
    along = [(i, i + per) for i in range(n - per)]

    def locals_after(first, count, moved):
        for _ in range(count):
            s, k = divmod(len(y_local), per_prompt)
            if s == prompts:
                break
            _, act = tied(first, fronts[s][0])
            first = local_part(s, k, act)
            y_local.append(first)
            moved, _ = tied(moved, first)
        return moved

    for t in range(parts + m - 2):
        at_k = jnp.clip(t - u, 0, parts - 1)
        leave = None
        for s in range(prompts - 1, -1, -1):
            if t < s * per_prompt:
                continue
            at_s = jnp.clip(at_k - s * per_prompt, 0, per_prompt - 1)
            own_t = lax.dynamic_index_in_dim(fronts[s][5], at_s, 0, keepdims=False)
            decay_t = lax.dynamic_index_in_dim(fronts[s][6], at_s, 0, keepdims=False)[:1]
            new = (decay_t * carry.astype(f32) + own_t).astype(bf16)
            leave = new if leave is None else jnp.where(at_k < (s + 1) * per_prompt, new, leave)
        moved = lax.ppermute(leave, "ctx", along)
        if t == 0:
            for s in range(1, prompts):
                _, sc = tied(leave, sc)
                fronts.append(list(front(s, dt_in)))
            moved, _ = tied(moved, fronts[-1][5])
        if t == 1:
            local, grow, payload = window(leave)
            blocks = [payload] + [trade(payload, k) for k in order[1:]]
            moved = locals_after(payload, 1, moved)
            keep, give = read(blocks, y_local[-1])
            got = trade(give, bits[0])
            moved = locals_after(give, 1, moved)
        if t == 2:
            for b in bits[1:]:
                both = (keep.astype(f32) + got.astype(f32)).astype(bf16)
                keep, give = jnp.split(both, 2)
                got = trade(give, b)
            _, gate_late = tied(give, gate_z)
            z_other = other_group(gate_late, gwidth)
            moved = locals_after(give, 1, moved)
        if t == 3:
            moved = locals_after(leave, 1, moved)
            _, keep = tied(y_local[-1], keep)
            hidden = finish([keep, got], local, grow)
            moved, _ = tied(moved, hidden)
            if per == 2:
                moved, _ = tied(moved, z_other)
        if t == 4:
            around = {0: hidden}
            for b in reversed(bits):
                around.update({k | b: trade(part, b) for k, part in around.items()})
            around = [around[k] for k in order]
            for got in around:
                moved, _ = tied(moved, got)
        if t == 5:
            _, around[0] = tied(leave, around[0])
            product = project(around)
            terms = lax.all_to_all(product, "tp", 0, 0)
        if t == per_prompt + m - 2:
            outs.append(back(0, leave))
            moved, _ = tied(moved, outs[0][0])
        if t == parts + m - 3:
            moved, _ = tied(moved, product)
        carry = moved
        arrived.append(carry)
    while len(y_local) < parts:
        done = len(y_local)
        y_local.append(local_part(done // per_prompt, done % per_prompt, fronts[done // per_prompt][0]))

    layer_out = jnp.sum(terms, axis=0).astype(bf16)
    for s in range(1, prompts):
        outs.append(back(s, carry))
    full_outs = []
    for out in outs:
        if per == 1:
            full_outs.append(out[0])
            continue
        given = swap(out[1])
        _, kept = tied(layer_out, out[0])
        full_outs.append(in_order(kept, given, 1))
    return (jnp.stack(full_outs), layer_out)


def solution(mesh):
    in_specs = (
        P(None, "ctx", "tp"),
        P(None, "ctx", "tp"),
        P(None, "ctx", "tp", None),
        P(None, "tp", "ctx"),
        P("tp"),
        P("tp"),
        P("tp"),
        P(None, "tp"),
        P(None, "tp", None),
        P("tp"),
        P("tp", None),
        P("tp"),
        P(None, "tp", None, None),
        P(None, None, "tp"),
        P(None, None, "tp", None),
        P(),
        P(None, "ctx", "tp"),
        P(None, "ctx", "tp"),
        P(None, "ctx", "tp", None),
        P(None, "tp", "ctx"),
        P("ctx"),
        P("tp", "ctx"),
    )
    out_specs = (P(None, "ctx", "tp"), P(None, "tp", "ctx"))
    return jax.shard_map(shards, mesh=mesh, in_specs=in_specs, out_specs=out_specs, check_vma=False)
```

```python
import functools

import jax
import jax.numpy as jnp
from jax import lax
from jax.experimental import pallas as pl
from jax.experimental.pallas import tpu as pltpu
from jax.sharding import PartitionSpec as P

epsilon = 1e-05
highest = lax.Precision.HIGHEST
f32, bf16 = jnp.float32, jnp.bfloat16
lanes = 128
vmem = 40 * 1024 * 1024


def silu(v):
    return v * (1.0 / (1.0 + jnp.exp(-v)))


def softplus(v):
    return jnp.maximum(v, 0.0) + jnp.log1p(jnp.exp(-jnp.abs(v)))


def exact(a, b):
    return jnp.dot(a, b, precision=highest, preferred_element_type=f32)


def exact_t(a, b):
    return lax.dot_general(
        a, b, (((1,), (1,)), ((), ())), precision=highest, preferred_element_type=f32
    )


def one_pass(a, b):
    return jnp.dot(a, b, preferred_element_type=f32)


def halves(a):
    high = a.astype(bf16)
    return high, (a - high.astype(f32)).astype(bf16)


def three_pass(a, b):
    a_hi, a_lo = halves(a)
    b_hi, b_lo = halves(b)
    return one_pass(a_hi, b_hi) + (one_pass(a_lo, b_hi) + one_pass(a_hi, b_lo))


def spread_out(a, picks):
    high, low = halves(a)
    return one_pass(high, picks) + one_pass(low, picks)


def to_channels(columns, hd, first):
    row = lax.broadcasted_iota(jnp.int32, (lanes, columns), 0)
    col = lax.broadcasted_iota(jnp.int32, (lanes, columns), 1)
    return (row == col // hd + first).astype(bf16)


def joined(refs, c, axis=0):
    if len(refs) == 1:
        return refs[0][0]
    a, b = refs[0][0], refs[1][0]
    return jnp.concatenate([jnp.where(c == 0, a, b), jnp.where(c == 0, b, a)], axis=axis)


def convolved(scratch, rim, body, taps_ref, bias_ref):
    rows = body.shape[0]
    taps = taps_ref.shape[0]
    scratch[0:8] = rim
    scratch[8 : 8 + rows] = body
    total = bias_ref[...]
    for k in range(taps):
        start = 8 - (taps - 1) + k
        total = total + taps_ref[k : k + 1] * scratch[start : start + rows]
    return silu(total)


def front_kernel(per, hd, prompt, sc, *refs):
    x_refs, refs = refs[:per], refs[per:]
    bc_refs, refs = refs[:per], refs[per:]
    dt_refs, refs = refs[:per], refs[per:]
    (rim_x, rim_bc, col, cx, cbc, bx, bbc, start) = refs[:8]
    (act_o, bc_o, run_o, step_o, pack_o, own_o, dec_o, start_o) = refs[8:16]
    xs, bs, bt = refs[16:]
    half = pl.program_id(0)
    c, u = sc[0], sc[1]
    _, heads, rows = run_o.shape
    n = bt.shape[0]
    bw = act_o.shape[2]

    @pl.when(half == 0)
    def _():
        at = u * rows + lax.broadcasted_iota(jnp.int32, (heads, rows), 1)
        live = jnp.where(at < sc[2 + prompt], 1.0, 0.0)
        step = softplus(joined(dt_refs, c, 1) + col[:, 1:2]) * live
        i = lax.broadcasted_iota(jnp.int32, (rows, rows), 0)
        j = lax.broadcasted_iota(jnp.int32, (rows, rows), 1)
        run = exact(-col[:, 0:1] * step, (i <= j).astype(f32))
        to_end = jnp.exp(run[:, rows - 1 :] - run) * step
        run_o[0] = run
        step_o[0] = step
        pack_o[0] = jnp.transpose(jnp.concatenate([to_end, jnp.exp(run), run, step], axis=0))
        bc = convolved(bs, rim_bc[0], joined(bc_refs, c).astype(f32), cbc, bbc)
        bc_o[0] = bc
        bt[...] = jnp.transpose(bc[:, :n])

    act = convolved(xs, rim_x[0], joined(x_refs, c).astype(f32), cx, bx)
    act_o[0] = act
    first = half * (bw // hd)
    weighted = act * spread_out(pack_o[0], to_channels(bw, hd, first))
    own = three_pass(bt[...], weighted)
    decay = spread_out(pack_o[0, rows - 8 :, :], to_channels(bw, hd, first + heads))[7:8]
    dec_o[0] = jnp.broadcast_to(decay, (8, bw))

    @pl.when(u == 0)
    def _():
        begin = jnp.transpose(start[0])
        own_o[0] = own + decay * begin
        start_o[0] = begin.astype(bf16)

    @pl.when(u != 0)
    def _():
        own_o[0] = own
        start_o[0] = jnp.zeros(start_o.shape[1:], bf16)


def local_kernel(hd, at_part, act, bc, run, step, pack, skip, y_o, scores):
    half = pl.program_id(0) + at_part
    heads, rows = run.shape[1:]
    bw = act.shape[2]
    n = bc.shape[2] // 2

    scores[...] = exact_t(bc[0, :, n:], bc[0, :, :n])

    i = lax.broadcasted_iota(jnp.int32, (rows, rows), 0)
    j = lax.broadcasted_iota(jnp.int32, (rows, rows), 1)
    lower = i >= j
    lane = lax.broadcasted_iota(jnp.int32, (rows, lanes), 1)
    each = lanes // hd
    first = half * (bw // hd)

    def block(q, carry):
        at = pl.ds(pl.multiple_of(q * lanes, lanes), lanes)
        x = act[0, :, at]
        x_hi, x_lo = halves(x)
        y = skip[:, at] * x
        for e in range(each):
            h = first + q * each + e
            column = jnp.sum(jnp.where(lane == h + 2 * heads, pack[0], 0.0), axis=1, keepdims=True)
            gap = column - run[0, pl.ds(h, 1), :]
            mixing = jnp.exp(jnp.where(lower, gap, -1e30)) * (scores[...] * step[0, pl.ds(h, 1), :])
            m_hi, m_lo = halves(mixing)
            got = one_pass(m_hi, x_hi) + (one_pass(m_lo, x_hi) + one_pass(m_hi, x_lo))
            y = y + jnp.where(lane // hd == e, got, 0.0)
        y_o[0, :, at] = y
        return carry

    lax.fori_loop(0, bw // lanes, block, 0)


def back_kernel(per, hd, heads, sc, *refs):
    g_refs, refs = refs[:per], refs[per:]
    outs, mixed = refs[-1 - per : -1], refs[-1]
    rest = refs[: -1 - per]
    parts = (len(rest) - 3) // 2
    entry, (bc, pack, gain), local = rest[:parts], rest[parts : parts + 3], rest[parts + 3 :]
    token_block = pl.program_id(0)
    c = sc[0]
    _, n, bw = entry[0].shape
    gate = g_refs[0][0]
    if per == 2:
        gate = jnp.where(token_block == c, gate, g_refs[1][0])
    c_hi, c_lo = halves(bc[0, :, n:])
    total = None
    for k in range(parts):
        at = slice(k * bw, (k + 1) * bw)
        seen = one_pass(c_hi, entry[k][0]) + one_pass(c_lo, entry[k][0])
        grow = spread_out(pack[0], to_channels(bw, hd, heads + k * (bw // hd)))
        y = local[k][0] + grow * seen
        v = y * silu(gate[:, at].astype(f32))
        mixed[:, at] = v
        square = jnp.sum(v * v, axis=1, keepdims=True)
        total = square if total is None else total + square
    scale = lax.rsqrt(total / (parts * bw) + epsilon)
    out = (mixed[...] * scale * gain[...]).astype(bf16)
    if per == 1:
        outs[0][...] = out
        return

    @pl.when(token_block == c)
    def _():
        outs[0][...] = out

    @pl.when(token_block != c)
    def _():
        outs[1][...] = out


def rows_of(refs, i, at, c):
    a = refs[0][i][:, at[0]].astype(f32)
    if len(refs) == 1:
        return a
    b = refs[1][i][:, at[1]].astype(f32)
    return jnp.concatenate([jnp.where(c == 0, a, b), jnp.where(c == 0, b, a)], axis=0)


def window_kernel(per, hd, heads, sc, *refs):
    x_ref, bc_ref, refs = refs[0], refs[1], refs[2:]
    other, refs = refs[: per - 1], refs[per - 1 :]
    small, refs = refs[:per], refs[per:]
    *tails, last0, last1, par, cx, cbc, bx, bbc, local_o, grow_o, pay_o = refs
    c = sc[0]
    taps = cx.shape[0]
    steps, batch, gwidth = x_ref.shape
    pair = bc_ref.shape[2]
    ns = pair // 2
    rows = per * batch
    whole = slice(None)
    tail = sum(t[...].astype(f32) for t in tails)
    prompt = rows_of(small, steps, (whole, whole), c)
    body_x = [rows_of([x_ref, *other], i, (whole, slice(0, gwidth)), c) for i in range(steps)]
    body_bc = [
        rows_of([bc_ref, *other], i, (whole, slice(gwidth, gwidth + pair)), c) for i in range(steps)
    ]

    def window(lo, hi, body):
        out = []
        for j in range(taps - 1):
            first, second = tail[j : j + 1, lo:hi], tail[8 + j : 9 + j, lo:hi]
            out.append(jnp.where(prompt[:, :1] == 0.0, first, second))
        return out + body

    def conv(full, taps_ref, bias):
        acts = []
        for i in range(steps):
            total = bias
            for k in range(taps):
                total = total + taps_ref[k : k + 1] * full[i + k]
            acts.append(silu(total))
        return acts

    xd = conv(window(0, gwidth, body_x), cx, bx[...])
    mix = conv(window(gwidth, gwidth + pair, body_bc), cbc, bbc[...])
    rate, dtb, skip = par[0:1], par[1:2], par[2:3]
    step = [softplus(rows_of(small, i, (whole, whole), c) + dtb) for i in range(steps)]
    upto = []
    for i in range(steps):
        upto.append((upto[-1] if upto else 0.0) - rate * step[i])
    coef = [jnp.broadcast_to(skip, (8, lanes))]
    for i in range(steps):
        read = mix[i][:, ns:]
        pay_o[i * rows : (i + 1) * rows, :ns] = read
        pay_o[i * rows : (i + 1) * rows, ns:] = prompt
        grow_o[i * rows : (i + 1) * rows] = jnp.exp(upto[i])
        for j in range(i + 1):
            both = jnp.sum(read * mix[j][:, :ns], axis=1, keepdims=True)
            coef.append(both * (jnp.exp(upto[i] - upto[j]) * step[j]))
    wide = spread_out(jnp.concatenate(coef, axis=0), to_channels(gwidth, hd, c * heads))
    at = 8
    for i in range(steps):
        y = wide[0:1] * xd[i]
        for j in range(i + 1):
            y = y + wide[at : at + rows] * xd[j]
            at += rows
        local_o[i * rows : (i + 1) * rows] = y
    pay_o[steps * rows :, :ns] = jnp.zeros((8, ns), f32)
    pay_o[steps * rows :, ns:] = jnp.concatenate(
        [last0[0, 7:8], last1[0, 7:8], jnp.zeros((6, lanes), f32)], axis=0
    )


def read_kernel(hd, heads, order, sc, *refs):
    m = len(order)
    blocks, own, outs = refs[:m], refs[m:-2], refs[-2:]
    half = pl.program_id(0)
    _, ns, bw = own[0].shape
    u = sc[1]
    rows = blocks[0].shape[0] - 8
    after = jnp.zeros((8, lanes), f32)
    for k, block in zip(order[1:], blocks[1:]):
        after = after + jnp.where((u ^ k) > u, block[rows:, ns:], 0.0)
    spread = spread_out(jnp.exp(after), to_channels(bw, hd, 2 * heads + half * (bw // hd)))
    asked = jnp.concatenate([b[:rows, :ns] for b in blocks], axis=0)
    prompt = jnp.concatenate([b[:rows, ns : ns + 1] for b in blocks], axis=0)
    total = None
    for s in range(len(own)):
        c_hi, c_lo = halves(jnp.where(prompt == s, asked, 0.0))
        s_hi, s_lo = halves(own[s][0] * spread[s : s + 1])
        got = one_pass(c_hi, s_hi) + (one_pass(c_lo, s_hi) + one_pass(c_hi, s_lo))
        total = got if total is None else total + got
    outs[0][...] = total[: m // 2 * rows].astype(bf16)
    outs[1][...] = total[m // 2 * rows :].astype(bf16)


def finish_kernel(per, hd, heads, sc, *refs):
    m = 2
    sums, local, grow, z_ref, refs = refs[:m], refs[m], refs[m + 1], refs[m + 2], refs[m + 3 :]
    *other, gain, out_o = refs
    c = sc[0]
    steps = z_ref.shape[0]
    gwidth = out_o.shape[1]
    total = sums[0][...].astype(f32)
    for r in sums[1:]:
        total = total + r[...].astype(f32)
    y = spread_out(grow[...], to_channels(gwidth, hd, c * heads)) * total + local[...]
    at = (slice(None), slice(other[0].shape[2] - gwidth, None) if other else None)
    gate = jnp.concatenate([rows_of([z_ref, *other], i, at, c) for i in range(steps)], axis=0)
    v = y * silu(gate)
    scale = lax.rsqrt(jnp.mean(v * v, axis=1, keepdims=True) + epsilon)
    out_o[...] = (v * scale * gain[...]).astype(bf16)


def project_kernel(per, order, sc, *refs):
    m = len(order)
    mine, other, w, out_o = refs[:m], refs[m:-2], refs[-2], refs[-1]
    c, u = sc[0], sc[1]
    tp, steps, rows_tp, cols = out_o.shape
    a = jnp.concatenate([r[...] for r in mine], axis=0)
    gwidth = a.shape[1]
    if per == 2:
        b = jnp.concatenate([r[...] for r in other], axis=0)
        total = one_pass(jnp.where(c == 0, a, b), w[:gwidth])
        total = total + one_pass(jnp.where(c == 0, b, a), w[gwidth:])
    else:
        total = one_pass(a, w[...])
    rows = a.shape[0] // (m * steps)
    each = m // tp
    for place, k in enumerate(order):
        v = u ^ k
        at = pl.ds(pl.multiple_of(lax.rem(v, each) * rows, rows), rows)
        for i in range(steps):
            first = (place * steps + i) * rows
            out_o[v // each, i, at, :] = total[first : first + rows]


def params(limit=vmem):
    return pltpu.CompilerParams(vmem_limit_bytes=limit)


def cost(us):
    return pl.CostEstimate(flops=int(us * 1.1e9), bytes_accessed=int(us * 3e6), transcendentals=0)


def tied(first, then):
    return lax.optimization_barrier((first, then))


def shards(
    inner_x,
    gate_z,
    proj_bc,
    dt_raw,
    a_log,
    dt_bias,
    d_skip,
    conv_x,
    conv_bc,
    bias_x,
    bias_bc,
    norm_gain,
    init_state,
    init_conv_x,
    init_conv_bc,
    lengths,
    dec_x,
    dec_z,
    dec_bc,
    dec_dt,
    row_prompt,
    w_out,
):
    prompts, tokens, width = inner_x.shape
    groups, pair = proj_bc.shape[2:]
    ns = pair // 2
    heads = dt_raw.shape[1] // groups
    gwidth = width // groups
    hd = gwidth // heads
    taps = conv_x.shape[0]
    steps, batch = dec_x.shape[:2]
    cols = w_out.shape[1]
    n = lax.axis_size("ctx")
    tp = lax.axis_size("tp")
    assert groups in (1, 2) and n % groups == 0 and 4 * heads == lanes
    per = groups
    m = n // per
    device = lax.axis_index("ctx")
    u, c = device // per, device % per
    unit_tokens = per * tokens
    rows_u = per * batch
    per_prompt = 2
    bw = gwidth // per_prompt
    parts = prompts * per_prompt

    def mine(arr, axis):
        return lax.dynamic_index_in_dim(arr, c, axis, keepdims=False)

    def swap(arr):
        return lax.ppermute(arr, "ctx", [(i, i ^ 1) for i in range(n)])

    def in_order(own, other, axis):
        first = jnp.where(c == 0, own, other)
        second = jnp.where(c == 0, other, own)
        return jnp.concatenate([first, second], axis=axis)

    def other_group(arr, size):
        if per == 1:
            return None
        at = [0] * (arr.ndim - 1) + [(1 - c) * size]
        return swap(lax.dynamic_slice(arr, at, arr.shape[:-1] + (size,)))

    def pair_up(arr, gaxis, taxis):
        if per == 1:
            return jnp.squeeze(arr, gaxis)
        other = swap(lax.dynamic_index_in_dim(arr, 1 - c, gaxis, keepdims=False))
        return in_order(mine(arr, gaxis), other, taxis)

    def trade(arr, k):
        return lax.ppermute(arr, "ctx", [(i, (i // per ^ k) * per + i % per) for i in range(n)])

    assert m & (m - 1) == 0
    bits = [1 << b for b in range(m.bit_length() - 1)]
    order = [0]
    for b in reversed(bits):
        order = order + [k | b for k in order]
    order = sorted(order, key=lambda k: [k >> b & 1 for b in range(len(bits))])

    bc_flat = proj_bc.reshape(prompts, tokens, groups * pair)
    x_other = bc_other = None
    if per == 2:
        x_send = lax.dynamic_slice_in_dim(inner_x, (1 - c) * gwidth, gwidth, 2)
        x_other = swap(x_send)
        bc_other = other_group(bc_flat, pair)
    last_x = inner_x[:, tokens - taps + 1 :]
    last_bc = bc_flat[:, tokens - taps + 1 :]
    wide = gwidth + pair
    rim = jnp.zeros((prompts, taps - 1, wide), bf16)
    for g in range(per):
        pairs = [(v * per + per - 1, (v + 1) * per + g) for v in range(m - 1)]
        send = jnp.concatenate(
            [last_x[..., g * gwidth : (g + 1) * gwidth], last_bc[..., g * pair : (g + 1) * pair]],
            axis=-1,
        )
        got = lax.ppermute(send, "ctx", pairs)
        rim = jnp.where(c == g, got, rim)
    lengths_late = tied(x_send, lengths)[1] if per == 2 else lengths
    want = jnp.arange(8, dtype=jnp.int32)
    target = lengths_late[:, None] - (taps - 1) + want
    target = jnp.where(want < taps - 1, target, -1)
    places = device * tokens + jnp.arange(tokens, dtype=jnp.int32)
    hit = places[None, None, :] == target[:, :, None]
    same = jnp.arange(prompts)[:, None] == jnp.arange(prompts)[None, :]
    picker = (hit[:, :, None, :] & same[:, None, :, None]).astype(bf16)
    picker = picker.reshape(prompts * 8, prompts * tokens)
    tail_x = jnp.dot(picker, inner_x.reshape(-1, width), preferred_element_type=f32).astype(bf16)
    tail_bc = jnp.dot(
        picker, bc_flat.reshape(-1, groups * pair), preferred_element_type=f32
    ).astype(bf16)

    def tail_of(g):
        return jnp.concatenate(
            [
                lax.dynamic_slice_in_dim(tail_x, g * gwidth, gwidth, 1),
                lax.dynamic_slice_in_dim(tail_bc, g * pair, pair, 1),
            ],
            axis=1,
        )

    tails = tail_of(c)
    if per == 2:
        tails = tails + swap(tail_of(1 - c))
    dt_in = [dt_raw]
    if per == 2:
        given = lax.dynamic_slice_in_dim(dt_raw, (1 - c) * heads, heads, 1)
        dt_in.append(swap(given))

    rate = jnp.exp(mine(a_log.reshape(groups, heads), 0))
    dtb = mine(dt_bias.reshape(groups, heads), 0)
    skip = jnp.repeat(mine(d_skip.reshape(groups, heads), 0), hd)[None]
    gain = mine(norm_gain.reshape(groups, 1, gwidth), 0)
    col = jnp.pad(jnp.stack([rate, dtb], axis=1), ((0, 0), (0, lanes - 2)))
    cbc = conv_bc.reshape(taps, groups * pair)
    bbc = bias_bc.reshape(1, groups * pair)
    bx = bias_x.reshape(1, width)
    start_rim = jnp.concatenate(
        [
            mine(init_conv_x.reshape(prompts, taps - 1, groups, gwidth), 2),
            mine(init_conv_bc, 2),
        ],
        axis=-1,
    )
    rim = jnp.where(u == 0, start_rim, rim).astype(f32)
    rim = jnp.pad(rim, ((0, 0), (8 - (taps - 1), 0), (0, 0)))
    start = init_state.reshape(prompts, groups * gwidth, ns)
    sc = jnp.concatenate([jnp.stack([c, u]).astype(jnp.int32), lengths])

    x_in = [inner_x] + ([x_other] if per == 2 else [])
    bc_in = [bc_flat] + ([bc_other] if per == 2 else [])
    T = unit_tokens
    spec = pl.BlockSpec

    def front(s, dts):
        in_specs = [spec((1, tokens, bw), lambda k, sc: (s, 0, sc[0] * per_prompt + k))]
        in_specs += [spec((1, tokens, bw), lambda k, sc: (s, 0, k))] * (per - 1)
        in_specs += [spec((1, tokens, pair), lambda k, sc: (s, 0, sc[0]))]
        in_specs += [spec((1, tokens, pair), lambda k, sc: (s, 0, 0))] * (per - 1)
        in_specs += [spec((1, heads, tokens), lambda k, sc: (s, sc[0], 0))]
        in_specs += [spec((1, heads, tokens), lambda k, sc: (s, 0, 0))] * (per - 1)
        in_specs += [
            spec((1, 8, bw), lambda k, sc: (s, 0, k)),
            spec((1, 8, pair), lambda k, sc: (s, 0, 0)),
            spec((heads, lanes), lambda k, sc: (0, 0)),
            spec((taps, bw), lambda k, sc: (0, sc[0] * per_prompt + k)),
            spec((taps, pair), lambda k, sc: (0, sc[0])),
            spec((1, bw), lambda k, sc: (0, sc[0] * per_prompt + k)),
            spec((1, pair), lambda k, sc: (0, sc[0])),
            spec((1, bw, ns), lambda k, sc: (s, sc[0] * per_prompt + k, 0)),
        ]
        chunk = lambda k, sc: (k, 0, 0)
        whole = lambda k, sc: (0, 0, 0)
        return pl.pallas_call(
            functools.partial(front_kernel, per, hd, s),
            grid_spec=pltpu.PrefetchScalarGridSpec(
                num_scalar_prefetch=1,
                grid=(per_prompt,),
                in_specs=in_specs,
                out_specs=[
                    spec((1, T, bw), lambda k, sc: (0, 0, k)),
                    spec((1, T, pair), whole),
                    spec((1, heads, T), whole),
                    spec((1, heads, T), whole),
                    spec((1, T, lanes), whole),
                    spec((1, ns, bw), chunk),
                    spec((1, 8, bw), chunk),
                    spec((1, ns, bw), chunk),
                ],
                scratch_shapes=[
                    pltpu.VMEM((T + 8, bw), f32),
                    pltpu.VMEM((T + 8, pair), f32),
                    pltpu.VMEM((ns, T), f32),
                ],
            ),
            out_shape=[
                jax.ShapeDtypeStruct((1, T, gwidth), f32),
                jax.ShapeDtypeStruct((1, T, pair), f32),
                jax.ShapeDtypeStruct((1, heads, T), f32),
                jax.ShapeDtypeStruct((1, heads, T), f32),
                jax.ShapeDtypeStruct((1, T, lanes), f32),
                jax.ShapeDtypeStruct((per_prompt, ns, bw), f32),
                jax.ShapeDtypeStruct((per_prompt, 8, bw), f32),
                jax.ShapeDtypeStruct((per_prompt, ns, bw), bf16),
            ],
            compiler_params=params(),
            cost_estimate=cost(9),
            name="front",
        )(sc, *x_in, *bc_in, *dts, rim[..., :gwidth], rim[..., gwidth:], col, conv_x, cbc, bx, bbc, start)

    def local_part(s, k, act):
        _, bc, run, step, pack = fronts[s][:5]
        return pl.pallas_call(
            functools.partial(local_kernel, hd, k),
            grid=(1,),
            in_specs=[
                spec((1, T, bw), lambda i: (0, 0, k)),
                spec((1, T, pair), lambda i: (0, 0, 0)),
                spec((1, heads, T), lambda i: (0, 0, 0)),
                spec((1, heads, T), lambda i: (0, 0, 0)),
                spec((1, T, lanes), lambda i: (0, 0, 0)),
                spec((1, bw), lambda i: (0, k)),
            ],
            out_specs=spec((1, T, bw), lambda i: (0, 0, 0)),
            out_shape=jax.ShapeDtypeStruct((1, T, bw), f32),
            scratch_shapes=[pltpu.VMEM((T, T), f32)],
            compiler_params=params(),
            cost_estimate=cost(5),
            name="local",
        )(act, bc, run, step, pack, skip)

    fronts = [list(front(0, dt_in))]
    after_front = fronts[0][5]
    _, dec_x = tied(after_front, dec_x)
    _, dec_bc = tied(after_front, dec_bc)
    _, dec_z = tied(after_front, dec_z)
    _, dec_dt = tied(after_front, dec_dt)
    _, row_prompt = tied(after_front, row_prompt)
    dec_bc = dec_bc.reshape(steps, batch, groups * pair)
    small = jnp.concatenate(
        [
            jnp.pad(jnp.transpose(dec_dt, (0, 2, 1)), ((0, 0), (0, 0), (0, lanes - groups * heads))),
            jnp.broadcast_to(row_prompt.astype(f32)[None, :, None], (1, batch, lanes)),
        ],
        axis=0,
    )
    small = [small]
    dec_other = []
    if per == 2:
        small.append(swap(small[0]))
        dec_other = [
            swap(
                jnp.concatenate(
                    [
                        lax.dynamic_slice_in_dim(dec_x, (1 - c) * gwidth, gwidth, 2),
                        lax.dynamic_slice_in_dim(dec_bc, (1 - c) * pair, pair, 2),
                        lax.dynamic_slice_in_dim(dec_z, (1 - c) * gwidth, gwidth, 2),
                    ],
                    axis=2,
                )
            )
        ]
    _, tails = tied(after_front, tails)
    tails = [tails] + [trade(tails, k) for k in range(1, m)]
    par = jnp.pad(
        jnp.stack([jnp.exp(a_log), dt_bias, d_skip]), ((0, 5), (0, lanes - groups * heads))
    )
    asked_rows = steps * rows_u

    def full_spec(arr):
        return spec(arr.shape, lambda *_: (0,) * arr.ndim)

    def window(first):
        _, late = tied(first, par)
        last = spec((1, 8, lanes), lambda i, sc: (0, T // 8 - 1, 0))
        return pl.pallas_call(
            functools.partial(window_kernel, per, hd, heads),
            grid_spec=pltpu.PrefetchScalarGridSpec(
                num_scalar_prefetch=1,
                grid=(1,),
                in_specs=[
                    spec((steps, batch, gwidth), lambda i, sc: (0, 0, sc[0])),
                    spec((steps, batch, pair), lambda i, sc: (0, 0, sc[0])),
                ]
                + [full_spec(a) for a in dec_other + small + tails]
                + [last, last, full_spec(par)]
                + [
                    spec((taps, gwidth), lambda i, sc: (0, sc[0])),
                    spec((taps, pair), lambda i, sc: (0, sc[0])),
                    spec((1, gwidth), lambda i, sc: (0, sc[0])),
                    spec((1, pair), lambda i, sc: (0, sc[0])),
                ],
                out_specs=[
                    spec((asked_rows, gwidth), lambda i, sc: (0, 0)),
                    spec((asked_rows, lanes), lambda i, sc: (0, 0)),
                    spec((asked_rows + 8, ns + lanes), lambda i, sc: (0, 0)),
                ],
            ),
            out_shape=[
                jax.ShapeDtypeStruct((asked_rows, gwidth), f32),
                jax.ShapeDtypeStruct((asked_rows, lanes), f32),
                jax.ShapeDtypeStruct((asked_rows + 8, ns + lanes), f32),
            ],
            compiler_params=params(),
            cost_estimate=cost(2),
            name="window",
        )(sc, dec_x, dec_bc, *dec_other, *small, *tails, fronts[0][4], fronts[1][4], late,
          conv_x, cbc, bx, bbc)

    def read(blocks, first):
        _, blocks[0] = tied(first, blocks[0])
        return pl.pallas_call(
            functools.partial(read_kernel, hd, heads, order),
            grid_spec=pltpu.PrefetchScalarGridSpec(
                num_scalar_prefetch=1,
                grid=(per_prompt,),
                in_specs=[full_spec(b) for b in blocks]
                + [spec((1, ns, bw), lambda k, sc: (k, 0, 0))] * prompts,
                out_specs=[spec((m // 2 * asked_rows, bw), lambda k, sc: (0, k))] * 2,
            ),
            out_shape=[jax.ShapeDtypeStruct((m // 2 * asked_rows, gwidth), bf16)] * 2,
            compiler_params=params(),
            cost_estimate=cost(4),
            name="read",
        )(sc, *blocks, *[f[5] for f in fronts])

    def finish(sums, local, grow):
        return pl.pallas_call(
            functools.partial(finish_kernel, per, hd, heads),
            grid_spec=pltpu.PrefetchScalarGridSpec(
                num_scalar_prefetch=1,
                grid=(1,),
                in_specs=[full_spec(a) for a in (*sums, local, grow)]
                + [spec((steps, batch, gwidth), lambda i, sc: (0, 0, sc[0]))]
                + [full_spec(a) for a in dec_other + [gain]],
                out_specs=spec((asked_rows, gwidth), lambda i, sc: (0, 0)),
            ),
            out_shape=jax.ShapeDtypeStruct((asked_rows, gwidth), bf16),
            compiler_params=params(),
            cost_estimate=cost(3),
            name="finish",
        )(sc, *sums, local, grow, dec_z, *dec_other, gain)

    def project(blocks):
        others = [swap(b) for b in blocks] if per == 2 else []
        cb = min(256, cols)
        return pl.pallas_call(
            functools.partial(project_kernel, per, order),
            grid_spec=pltpu.PrefetchScalarGridSpec(
                num_scalar_prefetch=1,
                grid=(cols // cb,),
                in_specs=[full_spec(b) for b in blocks + others]
                + [spec((width, cb), lambda i, sc: (0, i))],
                out_specs=spec((tp, steps, m * rows_u // tp, cb), lambda i, sc: (0, 0, 0, i)),
            ),
            out_shape=jax.ShapeDtypeStruct((tp, steps, m * rows_u // tp, cols), f32),
            compiler_params=params(60 * 1024 * 1024),
            cost_estimate=cost(6),
            name="project",
        )(sc, *blocks, *others, w_out)

    arrived, y_local, outs = [], [], []

    def back(s, first):
        entry = []
        for k in range(s * per_prompt, (s + 1) * per_prompt):
            e = fronts[s][7][k % per_prompt]
            for v in range(1, m):
                e = jnp.where(u == v, arrived[k + v - 1], e)
            entry.append(e)
        _, pack = tied(first, fronts[s][4])
        z_in = [gate_z] + ([z_other] if per == 2 else [])
        z_specs = [spec((1, tokens, gwidth), lambda j, sc: (s, 0, sc[0]))]
        z_specs += [spec((1, tokens, gwidth), lambda j, sc: (s, 0, 0))] * (per - 1)
        return pl.pallas_call(
            functools.partial(back_kernel, per, hd, heads),
            grid_spec=pltpu.PrefetchScalarGridSpec(
                num_scalar_prefetch=1,
                grid=(per,),
                in_specs=z_specs
                + [spec((1, ns, bw), lambda j, sc: (0, 0, 0))] * per_prompt
                + [
                    spec((1, tokens, pair), lambda j, sc: (0, j, 0)),
                    spec((1, tokens, lanes), lambda j, sc: (0, j, 0)),
                    spec((1, gwidth), lambda j, sc: (0, 0)),
                ]
                + [spec((1, tokens, bw), lambda j, sc: (0, j, 0))] * per_prompt,
                out_specs=[spec((tokens, gwidth), lambda j, sc: (0, 0))] * per,
                scratch_shapes=[pltpu.VMEM((tokens, gwidth), f32)],
            ),
            out_shape=[jax.ShapeDtypeStruct((tokens, gwidth), bf16)] * per,
            compiler_params=params(60 * 1024 * 1024),
            cost_estimate=cost(5),
            name="back",
        )(
            sc,
            *z_in,
            *[e[None] for e in entry],
            fronts[s][1],
            pack,
            gain,
            *y_local[s * per_prompt : (s + 1) * per_prompt],
        )

    carry = jnp.zeros((ns, bw), bf16)
    along = [(i, i + per) for i in range(n - per)]

    def locals_after(first, count, moved):
        for _ in range(count):
            s, k = divmod(len(y_local), per_prompt)
            if s == prompts:
                break
            _, act = tied(first, fronts[s][0])
            first = local_part(s, k, act)
            y_local.append(first)
            moved, _ = tied(moved, first)
        return moved

    for t in range(parts + m - 2):
        at_k = jnp.clip(t - u, 0, parts - 1)
        leave = None
        for s in range(prompts - 1, -1, -1):
            if t < s * per_prompt:
                continue
            at_s = jnp.clip(at_k - s * per_prompt, 0, per_prompt - 1)
            own_t = lax.dynamic_index_in_dim(fronts[s][5], at_s, 0, keepdims=False)
            decay_t = lax.dynamic_index_in_dim(fronts[s][6], at_s, 0, keepdims=False)[:1]
            new = (decay_t * carry.astype(f32) + own_t).astype(bf16)
            leave = new if leave is None else jnp.where(at_k < (s + 1) * per_prompt, new, leave)
        if t == 1:
            local, grow, payload = window(leave)
            blocks = [payload] + [trade(payload, k) for k in order[1:]]
            _, leave = tied(payload, leave)
        moved = lax.ppermute(leave, "ctx", along)
        if t == 0:
            for s in range(1, prompts):
                _, sc = tied(leave, sc)
                fronts.append(list(front(s, dt_in)))
            moved, _ = tied(moved, fronts[-1][5])
        if t == 1:
            moved = locals_after(payload, 1, moved)
            keep, give = read(blocks, y_local[-1])
            got = trade(give, bits[0])
            moved = locals_after(give, 1, moved)
        if t == 2:
            for b in bits[1:]:
                both = (keep.astype(f32) + got.astype(f32)).astype(bf16)
                keep, give = jnp.split(both, 2)
                got = trade(give, b)
            _, gate_late = tied(give, gate_z)
            z_other = other_group(gate_late, gwidth)
            moved = locals_after(give, 1, moved)
        if t == 3:
            moved = locals_after(leave, 1, moved)
            _, keep = tied(y_local[-1], keep)
            hidden = finish([keep, got], local, grow)
            moved, _ = tied(moved, hidden)
            if per == 2:
                moved, _ = tied(moved, z_other)
        if t == 4:
            around = {0: hidden}
            for b in reversed(bits):
                around.update({k | b: trade(part, b) for k, part in around.items()})
            around = [around[k] for k in order]
            for got in around:
                moved, _ = tied(moved, got)
        if t == 5:
            _, around[0] = tied(leave, around[0])
            product = project(around)
            terms = lax.all_to_all(product, "tp", 0, 0)
        if t == per_prompt + m - 2:
            outs.append(back(0, leave))
            moved, _ = tied(moved, outs[0][0])
        if t == parts + m - 3:
            moved, _ = tied(moved, product)
        carry = moved
        arrived.append(carry)
    while len(y_local) < parts:
        done = len(y_local)
        y_local.append(local_part(done // per_prompt, done % per_prompt, fronts[done // per_prompt][0]))

    layer_out = jnp.sum(terms, axis=0).astype(bf16)
    for s in range(1, prompts):
        outs.append(back(s, carry))
    full_outs = []
    for out in outs:
        if per == 1:
            full_outs.append(out[0])
            continue
        given = swap(out[1])
        _, kept = tied(layer_out, out[0])
        full_outs.append(in_order(kept, given, 1))
    return (jnp.stack(full_outs), layer_out)


def solution(mesh):
    in_specs = (
        P(None, "ctx", "tp"),
        P(None, "ctx", "tp"),
        P(None, "ctx", "tp", None),
        P(None, "tp", "ctx"),
        P("tp"),
        P("tp"),
        P("tp"),
        P(None, "tp"),
        P(None, "tp", None),
        P("tp"),
        P("tp", None),
        P("tp"),
        P(None, "tp", None, None),
        P(None, None, "tp"),
        P(None, None, "tp", None),
        P(),
        P(None, "ctx", "tp"),
        P(None, "ctx", "tp"),
        P(None, "ctx", "tp", None),
        P(None, "tp", "ctx"),
        P("ctx"),
        P("tp", "ctx"),
    )
    out_specs = (P(None, "ctx", "tp"), P(None, "tp", "ctx"))
    return jax.shard_map(shards, mesh=mesh, in_specs=in_specs, out_specs=out_specs, check_vma=False)
```
